256 devices in a mesh: ctx: 32 (over z, x), head: 8 (over y, core).
Axes of the slice: x: 4, y: 4, z: 8, core: 2. Of those that a mesh axis runs over, the one named last changes fastest.
Arguments:
- query: bfloat16 [8192, 2048], P('ctx', 'head'), may hold values from -6.5 to 6.5
- key: bfloat16 [8192, 2048], P('ctx', 'head'), may hold values from -6.5 to 6.5
- value: bfloat16 [8192, 2048], P('ctx', 'head'), may hold values from -6 to 6
- householder: bfloat16 [8192, 2048], P('ctx', 'head'), may hold values from -4 to 4, as said below
- cotangent: bfloat16 [8192, 2048], P('ctx', 'head'), may hold values from -6 to 6
- w_query: bfloat16 [4096, 2048], P(None, 'head'), may hold values from -0.09375 to 0.09375
- w_key: bfloat16 [4096, 2048], P(None, 'head'), may hold values from -0.09375 to 0.09375
- w_value: bfloat16 [4096, 2048], P(None, 'head'), may hold values from -0.09375 to 0.09375
Outputs:
- input_grad: float32 [8192, 4096], P('ctx', 'head')
The draws below stay inside these ranges and needn't reach their ends.
Inputs may be any that keep to these rules, and one draw needn't show every extreme that they name: `householder`: no token has a head whose vector is zero.
All inputs are finite; a program needn't handle non-finite values.
Results may differ from the reference program's by a relative error of at most 0.01705.
Values may be sent and summed in bfloat16 or wider, within the bound.
A program may use at most 128 MiB of HBM per device.

```python
import jax
import jax.numpy as jnp
from jax import lax

D = 4096
HEADS = 16
HEAD_DIM = 128
TOK_DEV = 256
TOKENS = 8192


def draw_query(key, part):
    key = jax.random.fold_in(key, 1)
    result_draw = jnp.clip(jax.random.normal(key, (TOKENS, HEADS, HEAD_DIM), jnp.float32), -4.0, 4.0)
    return result_draw.reshape(TOKENS, HEADS * HEAD_DIM).astype(jnp.bfloat16)


def draw_key(key, part):
    key = jax.random.fold_in(key, 2)
    result_draw = jnp.clip(jax.random.normal(key, (TOKENS, HEADS, HEAD_DIM), jnp.float32), -4.0, 4.0)
    return result_draw.reshape(TOKENS, HEADS * HEAD_DIM).astype(jnp.bfloat16)


def draw_householder(key, part):
    key = jax.random.fold_in(key, 3)
    result_draw = jnp.clip(jax.random.normal(key, (TOKENS, HEADS, HEAD_DIM), jnp.float32), -4.0, 4.0)
    return result_draw.reshape(TOKENS, HEADS * HEAD_DIM).astype(jnp.bfloat16)


def levels(own_key, extent, shards, least, top_value):
    def one(dim, shards_of):
        steps = jax.random.uniform(jax.random.fold_in(jax.random.fold_in(own_key, 6), dim), (shards_of,), jnp.float32, least / len(shards), top_value / len(shards))
        return jnp.repeat(jnp.exp(steps), extent[dim] // shards_of).reshape((-1,) + (1,) * (len(extent) - dim - 1))

    gain = one(*shards[0])
    for cut in shards[1:]:
        gain = gain * one(*cut)
    return gain


def gaussian(rng, shape, width, limit, cuts=(), held_as=jnp.bfloat16):
    drawn = width * jax.random.normal(rng, shape, jnp.float32)
    if cuts:
        drawn = drawn * levels(rng, shape, cuts, -0.22, 0.18)
    return jnp.clip(drawn, -limit, limit).astype(held_as)


def setup_inputs(seed: int = 0) -> dict:
    key_list = jax.random.split(jax.random.key(seed), 9)
    return {
        "query": draw_query(jax.random.fold_in(key_list[8], 71), 0),
        "key": draw_key(jax.random.fold_in(key_list[8], 71), 0),
        "value": gaussian(key_list[2], (TOKENS, HEADS * HEAD_DIM), 1.0, 6.0, ((0, 32), (1, 8))),
        "householder": draw_householder(jax.random.fold_in(key_list[8], 71), 0),
        "cotangent": gaussian(key_list[4], (TOKENS, HEADS * HEAD_DIM), 1.0, 6.0, ((0, 32), (1, 8))),
        "w_query": gaussian(key_list[5], (D, HEADS * HEAD_DIM), D ** -0.5, 0.09375, ((1, 8),)),
        "w_key": gaussian(key_list[6], (D, HEADS * HEAD_DIM), D ** -0.5, 0.09375, ((1, 8),)),
        "w_value": gaussian(key_list[7], (D, HEADS * HEAD_DIM), D ** -0.5, 0.09375, ((1, 8),)),
    }


precise_setting = lax.Precision.HIGHEST

def head_major(tensor, head_count):
    return tensor.reshape(tensor.shape[0], head_count, -1).transpose(1, 0, 2)

def householder_block(householder, head_count):
    vectors = head_major(householder.astype(jnp.float32), head_count)
    reflect_directions = vectors * lax.rsqrt(lax.optimization_barrier(jnp.sum(vectors * vectors, axis=-1, keepdims=True)) + 1e-06)
    row_total = reflect_directions.shape[1]
    head_width = reflect_directions.shape[2]
    gram_matrix = jnp.einsum('jsi,jri->jsr', reflect_directions, reflect_directions, precision=precise_setting)
    strict = jnp.tril(jnp.ones((row_total, row_total), dtype=bool), -1)
    lower_mat = jnp.eye(row_total, dtype=jnp.float32) + 2.0 * jnp.where(strict, gram_matrix, 0.0)
    solver = jax.vmap(lambda tri_mat, rhs_mat: jax.scipy.linalg.solve_triangular(tri_mat, rhs_mat, lower=True, unit_diagonal=True))
    update_terms = 2.0 * solver(lower_mat, reflect_directions)
    product = jnp.eye(head_width, dtype=jnp.float32) - jnp.einsum('hld,hle->hde', update_terms, reflect_directions, precision=precise_setting)
    return (reflect_directions, update_terms, product)

def turn_forward(value_rows, reflect_directions, update_terms, prefix_mat):
    row_total = value_rows.shape[1]
    inclusive_mask = jnp.tril(jnp.ones((row_total, row_total), dtype=bool))
    reflect_coefficients = jnp.where(inclusive_mask, jnp.einsum('otu,oku->otk', value_rows, reflect_directions, precision=precise_setting), 0.0)
    within_block_part = value_rows - jnp.einsum('xvw,xws->xvs', reflect_coefficients, update_terms, precision=precise_setting)
    return jnp.einsum('hie,hde->hid', within_block_part, prefix_mat, precision=precise_setting)

def turn_backward(grad_rows, reflect_directions, update_terms, prefix_mat):
    row_total = grad_rows.shape[1]
    inclusive_mask = jnp.tril(jnp.ones((row_total, row_total), dtype=bool))
    reflected_rows = jnp.einsum('hid,hde->hie', grad_rows, prefix_mat, precision=precise_setting)
    reflect_coefficients = jnp.where(inclusive_mask, jnp.einsum('hie,hme->him', reflected_rows, update_terms, precision=precise_setting), 0.0)
    return reflected_rows - jnp.einsum('xvw,xws->xvs', reflect_coefficients, reflect_directions, precision=precise_setting)

def reference(query, key, value, householder, cotangent, w_query, w_key, w_value):
    block_total = TOKENS // TOK_DEV
    width_all = HEADS * HEAD_DIM

    def to_blocks(tensor):
        return tensor.reshape(block_total, TOK_DEV, width_all)
    start_mat = jnp.broadcast_to(jnp.eye(HEAD_DIM, dtype=jnp.float32), (HEADS, HEAD_DIM, HEAD_DIM))

    def forward_step(prefix_mat, pieces):
        hh_piece, q_piece, k_piece = pieces
        reflect_directions, update_terms, product = householder_block(hh_piece, HEADS)
        q_turned = turn_forward(head_major(q_piece.astype(jnp.float32), HEADS), reflect_directions, update_terms, prefix_mat).astype(jnp.bfloat16)
        k_turned = turn_forward(head_major(k_piece.astype(jnp.float32), HEADS), reflect_directions, update_terms, prefix_mat).astype(jnp.bfloat16)
        following = jnp.einsum('hde,hef->hdf', prefix_mat, product, precision=precise_setting)
        return (following, (q_turned, k_turned, reflect_directions, update_terms, prefix_mat))
    _, (q_blocks, k_blocks, dir_blocks, upd_blocks, pre_blocks) = lax.scan(forward_step, start_mat, (to_blocks(householder), to_blocks(query), to_blocks(key)))
    q_heads = q_blocks.transpose(1, 0, 2, 3).reshape(HEADS, TOKENS, HEAD_DIM)
    k_heads = k_blocks.transpose(1, 0, 2, 3).reshape(HEADS, TOKENS, HEAD_DIM)
    v_heads = head_major(value, HEADS)
    d_heads = head_major(cotangent, HEADS)
    scale_factor = HEAD_DIM ** (-0.5)
    positions = jnp.arange(TOKENS)
    causal = positions[None, :] <= positions[:, None]

    def one_head(operands):
        q_one, k_one, v_one, d_one = operands
        scores = jnp.dot(q_one.astype(jnp.float32), k_one.T.astype(jnp.float32), preferred_element_type=jnp.float32) * scale_factor
        masked = jnp.where(causal, scores, -jnp.inf)
        log_total = jax.nn.logsumexp(masked, axis=1)
        soft_weights = jnp.where(causal, jnp.exp(scores - log_total[:, None]), 0.0)
        weights_low = soft_weights.astype(jnp.bfloat16)
        attended = jnp.dot(weights_low.astype(jnp.float32), v_one.astype(jnp.float32), preferred_element_type=jnp.float32)
        delta_row = lax.optimization_barrier(jnp.sum(d_one.astype(jnp.float32) * attended, axis=1))
        grad_weights = jnp.dot(d_one.astype(jnp.float32), v_one.T.astype(jnp.float32), preferred_element_type=jnp.float32)
        grad_scores = (soft_weights * (grad_weights - delta_row[:, None])).astype(jnp.bfloat16)
        grad_q = jnp.dot(grad_scores.astype(jnp.float32), k_one.astype(jnp.float32), preferred_element_type=jnp.float32) * scale_factor
        grad_k = jnp.dot(grad_scores.T.astype(jnp.float32), q_one.astype(jnp.float32), preferred_element_type=jnp.float32) * scale_factor
        grad_v = jnp.dot(weights_low.T.astype(jnp.float32), d_one.astype(jnp.float32), preferred_element_type=jnp.float32)
        return (grad_q, grad_k, grad_v)
    gq_heads, gk_heads, gv_heads = lax.map(one_head, (q_heads, k_heads, v_heads, d_heads))

    def back_blocks(tensor):
        return tensor.reshape(HEADS, block_total, TOK_DEV, HEAD_DIM).transpose(1, 0, 2, 3)

    def back_one(pieces):
        gq_piece, gk_piece, reflect_directions, update_terms, prefix_mat = pieces
        return (turn_backward(gq_piece, reflect_directions, update_terms, prefix_mat), turn_backward(gk_piece, reflect_directions, update_terms, prefix_mat))
    gq_back, gk_back = lax.map(back_one, (back_blocks(gq_heads), back_blocks(gk_heads), dir_blocks, upd_blocks, pre_blocks))

    def rows_of(tensor):
        return tensor.transpose(0, 2, 1, 3).reshape(TOKENS, width_all)
    grad_query = rows_of(gq_back).astype(jnp.bfloat16)
    grad_key = rows_of(gk_back).astype(jnp.bfloat16)
    grad_value = gv_heads.transpose(1, 0, 2).reshape(TOKENS, width_all).astype(jnp.bfloat16)
    input_grad = jnp.dot(grad_query.astype(jnp.float32), w_query.T.astype(jnp.float32), preferred_element_type=jnp.float32)
    input_grad = input_grad + jnp.dot(grad_key.astype(jnp.float32), w_key.T.astype(jnp.float32), preferred_element_type=jnp.float32)
    input_grad = input_grad + jnp.dot(grad_value.astype(jnp.float32), w_value.T.astype(jnp.float32), preferred_element_type=jnp.float32)
    return input_grad
```

```python
import functools
import math

import jax
import jax.numpy as jnp
from jax import lax
from jax.experimental import pallas as pl
from jax.experimental.pallas import tpu as pltpu
from jax.sharding import PartitionSpec as P

MESH = pl.DeviceIdType.MESH
BF = jnp.bfloat16
F32 = jnp.float32
ROWS = 256
HD = 128
NZ, NX = 8, 4
SCALE = HD**-0.5
SCALE2 = SCALE * math.log2(math.e)
VMEM_BYTES = 56 * 1024 * 1024
LOW = -1e30


def nn(a, b):
    return lax.dot_general(a, b, (((1,), (0,)), ((), ())), preferred_element_type=F32)


def nt(a, b):
    return lax.dot_general(a, b, (((1,), (1,)), ((), ())), preferred_element_type=F32)


def split(a):
    high = a.astype(BF)
    return high, (a - high.astype(F32)).astype(BF)


def nn3(a, b):
    ah, al = split(a)
    bh, bl = split(b)
    return nn(ah, bh) + (nn(al, bh) + nn(ah, bl))


def nt3(a, b):
    ah, al = split(a)
    bh, bl = split(b)
    return nt(ah, bh) + (nt(al, bh) + nt(ah, bl))


def iotas(shape):
    return lax.broadcasted_iota(jnp.int32, shape, 0), lax.broadcasted_iota(jnp.int32, shape, 1)


def identity():
    row, col = iotas((HD, HD))
    return jnp.where(row == col, 1.0, 0.0).astype(F32)


def place():
    me = lax.axis_index("ctx")
    return me // NX, me % NX


def meet(peers, axis):
    barrier = pltpu.get_barrier_semaphore()
    for peer in peers:
        pl.semaphore_signal(barrier, inc=1, device_id={axis: peer}, device_id_type=MESH)
    pl.semaphore_wait(barrier, len(peers))


def send(src, dst, send_sem, recv_sem, peer, axis="ctx"):
    return pltpu.make_async_remote_copy(
        src_ref=src,
        dst_ref=dst,
        send_sem=send_sem,
        recv_sem=recv_sem,
        device_id={axis: peer},
        device_id_type=MESH,
    )


def reflectors(hh, units, updates, products, lowers, inverses):
    row, col = iotas((HD, HD))
    chunks = [(a, b, slice(b * HD, (b + 1) * HD)) for a in range(2) for b in range(2)]
    for i, (a, b, rows) in enumerate(chunks):
        vec = hh[rows, a * HD : (a + 1) * HD].astype(F32)
        unit = vec * lax.rsqrt(jnp.sum(vec * vec, axis=1, keepdims=True) + 1e-6)
        lower = 2.0 * jnp.where(row > col, nt3(unit, unit), 0.0)
        units[a, rows] = unit
        lowers[i] = lower
        inverses[i] = identity() - jnp.where(row // 2 == col // 2, lower, 0.0)

    def join(level, carry):
        row_part, col_part = lax.shift_right_logical(row, level), lax.shift_right_logical(col, level)
        pick = (row_part == col_part + 1) & ((col_part & 1) == 0)
        for i in range(4):
            inverse = inverses[i]
            inner = nn3(jnp.where(pick, lowers[i], 0.0), inverse)
            inverses[i] = inverse - nn3(inverse, inner)
        return carry

    lax.fori_loop(1, 7, join, 0)
    for i, (a, b, rows) in enumerate(chunks):
        unit, inverse = units[a, rows], inverses[i]
        updates[a, rows] = 2.0 * nn3(inverse, unit)
        turned = 2.0 * nt3(unit.T, inverse)
        products[a, b] = identity() - nn3(turned, unit)


def gather_kernel(
    hh, q, k, v, c,
    qg, cg, kg, vg, units, updates, prefixes,
    qs, ks, cs, vs, px, tz, qlocal, klocal, products, lowers, inverses, totals,
    zs, zr, xs, xr, ps, pr, ts, tr, os, orr,
):
    z, x = place()
    head = z // 4
    line = [(z + d) % NZ for d in range(1, NZ)]
    cross = [(x + d) % NX for d in range(1, NX)]
    other = NZ - 1 - z
    x_rows = pl.ds(pl.multiple_of(x * ROWS, ROWS), ROWS)
    meet([zz * NX + x for zz in line] + [z * NX + xx for xx in cross], "ctx")

    def line_copies(src, dst, i):
        return [
            send(src.at[zz // 4], dst.at[z], zs.at[i, d], zr.at[i, d], zz * NX + x)
            for d, zz in enumerate(line)
        ]

    def pair_copy(src, dst, i):
        return send(
            src.at[1 - head], dst.at[head, x_rows], os.at[i], orr.at[i], other * NX + x
        )

    def cross_copies(dst, slot, i):
        return [
            send(dst.at[slot, x_rows], dst.at[slot, x_rows], xs.at[i, d], xr.at[i, d], z * NX + xx)
            for d, xx in enumerate(cross)
        ]

    for part in range(2):
        cols = slice(part * HD, (part + 1) * HD)
        cs[part] = c[:, cols]
        vs[part] = v[:, cols]
    c_copies = line_copies(cs, cg, 0)
    v_pair = pair_copy(vs, vg, 0)
    v_pair.start()
    for copy in c_copies:
        copy.start()
    cg[z] = cs[head]
    vg[head, x_rows] = vs[head]
    v_cross = cross_copies(vg, head, 0)
    for copy in v_cross:
        copy.start()

    reflectors(hh, units, updates, products, lowers, inverses)
    for a in range(2):
        px[x, a] = nn3(products[a, 0], products[a, 1])
    p_cross = [
        send(px.at[x], px.at[x], ps.at[d], pr.at[d], z * NX + xx) for d, xx in enumerate(cross)
    ]
    for copy in p_cross:
        copy.start()

    v_pair.wait()
    v_cross2 = cross_copies(vg, 1 - head, 1)
    for copy in v_cross2:
        copy.start()

    row, col = iotas((HD, HD))
    for a in range(2):
        for b in range(2):
            rows = slice(b * HD, (b + 1) * HD)
            for src, dst in ((q, qlocal), (k, klocal)):
                part = src[rows, a * HD : (a + 1) * HD].astype(F32)
                coef = jnp.where(row >= col, nt3(part, units[a, rows]), 0.0)
                dst[a, rows] = part - nn3(coef, updates[a, rows])

    for copy in p_cross:
        copy.wait()
    for a in range(2):
        one = px[0, a]
        two = nn3(one, px[1, a])
        three = nn3(two, px[2, a])
        tz[z, a] = nn3(three, px[3, a])
        prefixes[a, 0] = jnp.where(
            x == 0, identity(), jnp.where(x == 1, one, jnp.where(x == 2, two, three))
        )
    t_line = [
        send(tz.at[z], tz.at[z], ts.at[d], tr.at[d], zz * NX + x) for d, zz in enumerate(line)
    ]
    for d in range(1, NZ):

        @pl.when(z + d < NZ)
        def _(d=d):
            t_line[d - 1].start()

    for d in range(1, NZ):

        @pl.when(z - d >= 0)
        def _(d=d):
            t_line[d - 1].wait_recv()

    for a in range(2):
        totals[a] = identity()

    def chain(j, carry):
        for a in range(2):
            totals[a] = nn3(totals[a], tz[j, a])
        return carry

    lax.fori_loop(0, z, chain, 0)
    for a in range(2):
        first = nn3(totals[a], prefixes[a, 0])
        second = nn3(first, products[a, 0])
        prefixes[a, 0] = first
        prefixes[a, 1] = second
        for b, prefix in enumerate((first, second)):
            rows = slice(b * HD, (b + 1) * HD)
            ks[a, rows] = nt3(klocal[a, rows], prefix).astype(BF)
            qs[a, rows] = nt3(qlocal[a, rows], prefix).astype(BF)

    k_pair = pair_copy(ks, kg, 1)
    k_pair.start()
    kg[head, x_rows] = ks[head]
    k_cross = cross_copies(kg, head, 2)
    for copy in k_cross:
        copy.start()
    q_copies = line_copies(qs, qg, 1)
    for copy in q_copies:
        copy.start()
    qg[z] = qs[head]
    k_pair.wait()
    k_cross2 = cross_copies(kg, 1 - head, 3)
    for copy in k_cross2:
        copy.start()
    for d in range(1, NZ):

        @pl.when(z + d < NZ)
        def _(d=d):
            t_line[d - 1].wait_send()

    for copy in c_copies + v_cross + v_cross2 + k_cross + q_copies + k_cross2:
        copy.wait()


def full_tile(n, low_row):
    in_low = n < NZ - 1 - low_row
    return jnp.where(in_low, low_row + 1 + n, n + 1), jnp.where(in_low, 0, 1)


def forward_kernel(qg, cg, kg, vg, top, total, delta, s_scr):
    z, x = place()
    low_row = jnp.minimum(z, NZ - 1 - z)
    top[...] = jnp.full(top.shape, LOW, F32)
    total[...] = jnp.zeros(total.shape, F32)
    delta[...] = jnp.zeros(delta.shape, F32)

    def join(row, peak, weight, moment):
        at = pl.ds(row, 1)
        old = top[at, :]
        new = jnp.maximum(old, peak)
        keep, take = jnp.exp2(old - new), jnp.exp2(peak - new)
        top[at, :] = new
        total[at, :] = total[at, :] * keep + weight * take
        delta[at, :] = delta[at, :] * keep + moment * take

    def full(n, carry):
        row, slot = full_tile(n, low_row)
        query, cot = qg[row], cg[row]
        peak = None
        for j in range(NX):
            rows = slice(j * ROWS, (j + 1) * ROWS)
            score = nt(kg[slot, rows], query) * SCALE2
            s_scr[rows] = score
            mine = jnp.max(score, axis=0, keepdims=True)
            peak = mine if peak is None else jnp.maximum(peak, mine)
        weight = moment = jnp.zeros((1, ROWS), F32)
        for j in range(NX):
            rows = slice(j * ROWS, (j + 1) * ROWS)
            p = jnp.exp2(s_scr[rows] - peak)
            weight = weight + jnp.sum(p, axis=0, keepdims=True)
            moment = moment + jnp.sum(p * nt(vg[slot, rows], cot), axis=0, keepdims=True)
        join(row, peak, weight, moment)
        return carry

    lax.fori_loop(0, NZ - 1, full, 0)

    def edge(n, carry):
        slot, j = n % 2, n // 2
        row = jnp.where(slot == 0, low_row, NZ - 1 - low_row)
        rows = pl.ds(pl.multiple_of(j * ROWS, ROWS), ROWS)
        key_at, query_at = iotas((ROWS, ROWS))
        live = key_at + j * ROWS <= query_at + x * ROWS
        score = jnp.where(live, nt(kg[slot, rows], qg[row]) * SCALE2, LOW)
        peak = jnp.max(score, axis=0, keepdims=True)
        p = jnp.where(live, jnp.exp2(score - peak), 0.0)
        moment = jnp.sum(p * nt(vg[slot, rows], cg[row]), axis=0, keepdims=True)
        join(row, peak, jnp.sum(p, axis=0, keepdims=True), moment)
        return carry

    lax.fori_loop(0, 2 * (x + 1), edge, 0)


def stats_kernel(top, total, delta, log_total, delta_row, held, ss, sr):
    z, x = place()
    half = z // 4
    peers = [(half * 4 + (z + d) % 4) * NX + x for d in range(1, 4)]
    meet(peers, "ctx")
    held[z % 4, 0] = top[...]
    held[z % 4, 1] = total[...]
    held[z % 4, 2] = delta[...]
    copies = [
        send(held.at[z % 4], held.at[z % 4], ss.at[d], sr.at[d], peer)
        for d, peer in enumerate(peers)
    ]
    for copy in copies:
        copy.start()
    for copy in copies:
        copy.wait()
    peak = held[0, 0]
    for i in range(1, 4):
        peak = jnp.maximum(peak, held[i, 0])
    weight = moment = jnp.zeros(peak.shape, F32)
    for i in range(4):
        take = jnp.exp2(held[i, 0] - peak)
        weight = weight + held[i, 1] * take
        moment = moment + held[i, 2] * take
    log_total[...] = peak + jnp.log2(weight)
    delta_row[...] = moment / weight


def backward_kernel(qg, cg, kg, vg, log_total, delta_row, dqt, dkv, kt, dq_acc, dk_acc, dv_acc):
    z, x = place()
    low_row = jnp.minimum(z, NZ - 1 - z)
    dq_acc[...] = jnp.zeros(dq_acc.shape, F32)
    dk_acc[...] = jnp.zeros(dk_acc.shape, F32)
    dv_acc[...] = jnp.zeros(dv_acc.shape, F32)
    for slot in range(2):
        for j in range(NX):
            rows = slice(j * ROWS, (j + 1) * ROWS)
            kt[slot, j] = kg[slot, rows].T

    def tile(row, slot, j, rows, live):
        key, query, cot = kg[slot, rows], qg[row], cg[row]
        at = pl.ds(row, 1)
        score = nt(key, query) * SCALE2 - log_total[at, :]
        if live is not None:
            score = jnp.where(live, score, LOW)
        p = jnp.exp2(score)
        grad = (p * (nt(vg[slot, rows], cot) - delta_row[at, :])).astype(BF)
        dv_acc[slot, rows] += nn(p.astype(BF), cot)
        dk_acc[slot, rows] += nn(grad, query)
        return nn(kt[slot, j], grad)

    def full(n, carry):
        row, slot = full_tile(n, low_row)
        total = None
        for j in range(NX):
            part = tile(row, slot, j, slice(j * ROWS, (j + 1) * ROWS), None)
            total = part if total is None else total + part
        dq_acc[row] += total
        return carry

    lax.fori_loop(0, NZ - 1, full, 0)

    def edge(n, carry):
        slot, j = n % 2, n // 2
        row = jnp.where(slot == 0, low_row, NZ - 1 - low_row)
        rows = pl.ds(pl.multiple_of(j * ROWS, ROWS), ROWS)
        key_at, query_at = iotas((ROWS, ROWS))
        live = key_at + j * ROWS <= query_at + x * ROWS
        dq_acc[row] += tile(row, slot, j, rows, live)
        return carry

    lax.fori_loop(0, 2 * (x + 1), edge, 0)
    dqt[...] = (dq_acc[...] * SCALE).astype(BF)
    dkv[:, :, :HD] = (dk_acc[...] * SCALE).astype(BF)
    dkv[:, :, HD:] = dv_acc[...].astype(BF)


def reduce_kernel(dqt, dkv, rq, own, given, rx, out, zs, zr, xs, xr, os, orr):
    z, x = place()
    head = z // 4
    line = [(z + d) % NZ for d in range(1, NZ)]
    cross = [(x + d) % NX for d in range(1, NX)]
    meet([zz * NX + x for zz in line] + [z * NX + xx for xx in cross], "ctx")

    def rows_of(xx):
        return pl.ds(pl.multiple_of(xx * ROWS, ROWS), ROWS)

    x_copies = [
        [
            send(
                dkv.at[slot, rows_of(xx)], rx.at[x, i], xs.at[i, d], xr.at[i, d], z * NX + xx
            )
            for d, xx in enumerate(cross)
        ]
        for i, slot in enumerate((1 - head, head))
    ]
    for copies in x_copies:
        for copy in copies:
            copy.start()
    z_copies = [
        send(dqt.at[zz], rq.at[z], zs.at[d], zr.at[d], zz * NX + x) for d, zz in enumerate(line)
    ]
    for copy in z_copies:
        copy.start()
    rq[z] = dqt[z]
    rx[x, 0] = dkv[1 - head, rows_of(x)]
    rx[x, 1] = dkv[head, rows_of(x)]

    def summed(i):
        return (rx[0, i].astype(F32) + rx[1, i].astype(F32)) + (
            rx[2, i].astype(F32) + rx[3, i].astype(F32)
        )

    for copy in x_copies[0]:
        copy.wait()
    out[...] = summed(0).astype(BF)
    pair = send(out, given, os.at[0], orr.at[0], (NZ - 1 - z) * NX + x)
    pair.start()
    for copy in x_copies[1]:
        copy.wait()
    own[...] = summed(1)
    pair.wait()
    for copy in z_copies:
        copy.wait()


def project_kernel(
    rq, own, given, units, updates, prefixes, wq, wk, wv,
    out,
    w, grads, kv, mine, theirs, relay, landed,
    ws, cs, cr, ys, yr,
):
    z, _ = place()
    head = z // 4
    me = lax.axis_index("head")
    y, core = me // 2, me % 2
    mate = y * 2 + 1 - core
    order = [(y + d) % 4 for d in (2, 1, 3)]
    meet([mate] + [yy * 2 + core for yy in order], "head")
    loads = [pltpu.make_async_copy(src, w.at[i], ws.at[i]) for i, src in enumerate((wq, wk, wv))]
    for load in loads:
        load.start()
    kv[head] = own[...]
    kv[1 - head] = given[...].astype(F32)
    row, col = iotas((HD, HD))
    for a in range(2):
        cols = slice(a * HD, (a + 1) * HD)
        total = rq[4 * a].astype(F32)
        for i in range(1, 4):
            total = total + rq[4 * a + i].astype(F32)
        total = total.T
        grads[2, :, cols] = kv[a, :, HD:].astype(BF)
        for b in range(2):
            rows = slice(b * HD, (b + 1) * HD)
            for i, part in enumerate((total[rows], kv[a, rows, :HD])):
                back = nn3(part, prefixes[a, b])
                coef = jnp.where(row >= col, nt3(back, updates[a, rows]), 0.0)
                grads[i, rows, cols] = (back - nn3(coef, units[a, rows])).astype(BF)
    for load in loads:
        load.wait()

    def columns(block):
        at = pl.ds(pl.multiple_of(block * 512, 512), 512)
        return (
            nt(grads[0], w[0, at, :]) + nt(grads[1], w[1, at, :]) + nt(grads[2], w[2, at, :])
        )

    blocks = order + [y]
    swaps = []
    for i, yy in enumerate(blocks):
        mine[i] = columns(yy * 2 + 1 - core).astype(BF)
        swap = send(mine.at[i], theirs.at[i], cs.at[i], cr.at[i], mate, "head")
        swap.start()
        swaps.append(swap)
    hops = []
    for i, yy in enumerate(blocks):
        part = columns(yy * 2 + core)
        swaps[i].wait()
        part = part + theirs[i].astype(F32)
        if i < 3:
            relay[i] = part.astype(BF)
            hop = send(relay.at[i], landed.at[i], ys.at[i], yr.at[i], yy * 2 + core, "head")
            hop.start()
            hops.append(hop)
    for hop in hops:
        hop.wait()
        part = part
    for i in range(3):
        part = part + landed[i].astype(F32)
    out[...] = part


def call(kernel, outs, scratch, collective, in_specs, **extra):
    vmem = pl.BlockSpec(memory_space=pltpu.VMEM)
    params = dict(vmem_limit_bytes=VMEM_BYTES)
    if collective is not None:
        params.update(collective_id=collective, has_side_effects=True)
    return pl.pallas_call(
        kernel,
        out_shape=[jax.ShapeDtypeStruct(s, t) for s, t in outs],
        in_specs=[vmem if s is None else pl.BlockSpec(memory_space=s) for s in in_specs],
        out_specs=[vmem] * len(outs),
        scratch_shapes=scratch,
        compiler_params=pltpu.CompilerParams(**params),
        **extra,
    )


def on_device(query, key, value, householder, cotangent, w_query, w_key, w_value):
    dma = pltpu.SemaphoreType.DMA
    lines = ((NZ, ROWS, HD), BF)
    keys = ((2, NX * ROWS, HD), BF)
    own = pltpu.VMEM((2, ROWS, HD), BF)
    own32 = pltpu.VMEM((2, ROWS, HD), F32)
    qg, cg, kg, vg, units, updates, prefixes = call(
        gather_kernel,
        [
            lines, lines, keys, keys,
            ((2, ROWS, HD), F32), ((2, ROWS, HD), F32), ((2, 2, HD, HD), F32),
        ],
        [
            own, own, own, own,
            pltpu.VMEM((NX, 2, HD, HD), F32), pltpu.VMEM((NZ, 2, HD, HD), F32), own32, own32,
            pltpu.VMEM((2, 2, HD, HD), F32), pltpu.VMEM((4, HD, HD), F32),
            pltpu.VMEM((4, HD, HD), F32), pltpu.VMEM((2, HD, HD), F32),
            dma((2, 7)), dma((2, 7)), dma((4, 3)), dma((4, 3)), dma((3,)), dma((3,)),
            dma((7,)), dma((7,)), dma((2,)), dma((2,)),
        ],
        0,
        [None] * 5,
    )(householder, query, key, value, cotangent)
    stat = ((NZ, ROWS), F32)
    top, total, delta = call(
        forward_kernel, [stat] * 3, [pltpu.VMEM((NX * ROWS, ROWS), F32)], None, [None] * 4
    )(qg, cg, kg, vg)
    log_total, delta_row = call(
        stats_kernel,
        [stat] * 2,
        [pltpu.VMEM((4, 3, NZ, ROWS), F32), dma((3,)), dma((3,))],
        1,
        [None] * 3,
    )(top, total, delta)
    acc = pltpu.VMEM((2, NX * ROWS, HD), F32)
    dqt, dkv = call(
        backward_kernel,
        [((NZ, HD, ROWS), BF), ((2, NX * ROWS, 2 * HD), BF)],
        [pltpu.VMEM((2, NX, HD, ROWS), BF), pltpu.VMEM((NZ, HD, ROWS), F32), acc, acc],
        None,
        [None] * 6,
    )(qg, cg, kg, vg, log_total, delta_row)
    block = (ROWS, 2 * HD)
    rq, mine, given = call(
        reduce_kernel,
        [((NZ, HD, ROWS), BF), (block, F32), (block, BF)],
        [
            pltpu.VMEM((NX, 2) + block, BF), pltpu.VMEM(block, BF),
            dma((7,)), dma((7,)), dma((2, 3)), dma((2, 3)), dma((1,)), dma((1,)),
        ],
        2,
        [None] * 2,
    )(dqt, dkv)
    (result,) = call(
        project_kernel,
        [((ROWS, 512), F32)],
        [
            pltpu.VMEM((3, 4096, ROWS), BF), pltpu.VMEM((3, ROWS, ROWS), BF),
            pltpu.VMEM((2,) + block, F32),
            pltpu.VMEM((4, ROWS, 512), BF), pltpu.VMEM((4, ROWS, 512), BF),
            pltpu.VMEM((3, ROWS, 512), BF), pltpu.VMEM((3, ROWS, 512), BF),
            dma((3,)), dma((4,)), dma((4,)), dma((3,)), dma((3,)),
        ],
        3,
        [None] * 6 + [pl.ANY] * 3,
    )(rq, mine, given, units, updates, prefixes, w_query, w_key, w_value)
    return result


def solution(mesh):
    return jax.shard_map(
        on_device,
        mesh=mesh,
        in_specs=(P("ctx", "head"),) * 5 + (P(None, "head"),) * 3,
        out_specs=P("ctx", "head"),
        check_vma=False,
    )
```

```python
import math

import jax
import jax.numpy as jnp
from jax import lax
from jax.experimental import pallas as pl
from jax.experimental.pallas import tpu as pltpu
from jax.sharding import PartitionSpec as P

MESH = pl.DeviceIdType.MESH
BF = jnp.bfloat16
F32 = jnp.float32
ROWS = 256
HD = 128
NZ, NX = 8, 4
SCALE = HD**-0.5
SCALE2 = SCALE * math.log2(math.e)
VMEM_BYTES = 56 * 1024 * 1024
LOW = -1e30


def nn(a, b):
    return lax.dot_general(a, b, (((1,), (0,)), ((), ())), preferred_element_type=F32)


def nt(a, b):
    return lax.dot_general(a, b, (((1,), (1,)), ((), ())), preferred_element_type=F32)


def split(a):
    high = a.astype(BF)
    return high, (a - high.astype(F32)).astype(BF)


def nn3(a, b):
    ah, al = split(a)
    bh, bl = split(b)
    return nn(ah, bh) + (nn(al, bh) + nn(ah, bl))


def nt3(a, b):
    ah, al = split(a)
    bh, bl = split(b)
    return nt(ah, bh) + (nt(al, bh) + nt(ah, bl))


def iotas(shape):
    return lax.broadcasted_iota(jnp.int32, shape, 0), lax.broadcasted_iota(jnp.int32, shape, 1)


def identity():
    row, col = iotas((HD, HD))
    return jnp.where(row == col, 1.0, 0.0).astype(F32)


def place():
    me = lax.axis_index("ctx")
    return me // NX, me % NX


def send(src, dst, send_sem, recv_sem, peer, axis="ctx"):
    return pltpu.make_async_remote_copy(
        src_ref=src,
        dst_ref=dst,
        send_sem=send_sem,
        recv_sem=recv_sem,
        device_id={axis: peer},
        device_id_type=MESH,
    )


def reflectors(hh, units, updates, products, lowers, inverses):
    row, col = iotas((HD, HD))
    chunks = [(a, b, slice(b * HD, (b + 1) * HD)) for a in range(2) for b in range(2)]
    for i, (a, b, rows) in enumerate(chunks):
        vec = hh[rows, a * HD : (a + 1) * HD].astype(F32)
        unit = vec * lax.rsqrt(jnp.sum(vec * vec, axis=1, keepdims=True) + 1e-6)
        lower = 2.0 * jnp.where(row > col, nt3(unit, unit), 0.0)
        units[a, rows] = unit
        lowers[i] = lower
        inverses[i] = identity() - jnp.where(row // 2 == col // 2, lower, 0.0)

    def join(level, carry):
        row_part, col_part = lax.shift_right_logical(row, level), lax.shift_right_logical(col, level)
        pick = (row_part == col_part + 1) & ((col_part & 1) == 0)
        for i in range(4):
            inverse = inverses[i]
            inner = nn3(jnp.where(pick, lowers[i], 0.0), inverse)
            inverses[i] = inverse - nn3(inverse, inner)
        return carry

    lax.fori_loop(1, 7, join, 0)
    for i, (a, b, rows) in enumerate(chunks):
        unit, inverse = units[a, rows], inverses[i]
        updates[a, rows] = 2.0 * nn3(inverse, unit)
        turned = 2.0 * nt3(unit.T, inverse)
        products[a, b] = identity() - nn3(turned, unit)


def rows_at(block):
    return pl.ds(pl.multiple_of(block * ROWS, ROWS), ROWS)


def whole_kernel(
    hh, q, k, v, c, wq, wk, wv,
    out,
    qg, cg, kg, vg, units, updates, prefixes,
    qs, ks, cs, vs, px, tz, qlocal, klocal, products, lowers, inverses, totals,
    s_scr, held, log_total, delta_row,
    kt, dq_acc, dk_acc, dv_acc, dqt, dkv, rq, rx, pair_out, kv,
    w, grads, mine, theirs, relay, landed,
    zs, zr, xs, xr, ps, pr, ts, tr, fs, fr, os, orr, ss, sr, ws, ms, mr, ys, yr,
):
    z, x = place()
    me = lax.axis_index("head")
    y, core = me // 2, me % 2
    mate = y * 2 + 1 - core
    head = z // 4
    low_row = jnp.minimum(z, NZ - 1 - z)
    other = NZ - 1 - z
    line = [(z + d) % NZ for d in range(1, NZ)]
    cross = [(x + d) % NX for d in range(1, NX)]
    order = [(y + d) % 4 for d in (2, 1, 3)]
    loads = [pltpu.make_async_copy(src, w.at[i], ws.at[i]) for i, src in enumerate((wq, wk, wv))]
    for load in loads:
        load.start()
    barrier = pltpu.get_barrier_semaphore()
    peers = [{"ctx": zz * NX + x} for zz in line] + [{"ctx": z * NX + xx} for xx in cross]
    peers = peers + [{"head": mate}] + [{"head": yy * 2 + core} for yy in order]
    for peer in peers:
        pl.semaphore_signal(barrier, inc=1, device_id=peer, device_id_type=MESH)
    pl.semaphore_wait(barrier, len(peers))

    def line_copy(src, dst, i, to, source):
        return send(src.at[to // 4], dst.at[source], zs.at[i, to], zr.at[i, source], to * NX + x)

    def line_start(src, dst, i):
        def step(d, carry):
            to = (z + d) % NZ

            @pl.when(z >= jnp.minimum(to, NZ - 1 - to))
            def _():
                line_copy(src, dst, i, to, z).start()

            return carry

        lax.fori_loop(1, NZ, step, 0)

    def line_wait_send(src, dst, i):
        def step(d, carry):
            to = (z + d) % NZ

            @pl.when(z >= jnp.minimum(to, NZ - 1 - to))
            def _():
                line_copy(src, dst, i, to, z).wait_send()

            return carry

        lax.fori_loop(1, NZ, step, 0)

    def pair_copy(src, dst, i):
        return send(
            src.at[1 - head], dst.at[head, rows_at(x)], os.at[i], orr.at[i], other * NX + x
        )

    def cross_copies(dst, slot, i):
        return [
            send(dst.at[slot, rows_at(x)], dst.at[slot, rows_at(x)], xs.at[i, d], xr.at[i, d], z * NX + xx)
            for d, xx in enumerate(cross)
        ]

    for part in range(2):
        cols = slice(part * HD, (part + 1) * HD)
        cs[part] = c[:, cols]
        vs[part] = v[:, cols]
    v_pair = pair_copy(vs, vg, 0)
    v_pair.start()
    line_start(cs, cg, 0)
    cg[z] = cs[head]
    vg[head, rows_at(x)] = vs[head]
    v_cross = cross_copies(vg, head, 0)
    for copy in v_cross:
        copy.start()

    reflectors(hh, units, updates, products, lowers, inverses)
    for a in range(2):
        px[x, a] = nn3(products[a, 0], products[a, 1])
    p_cross = [
        send(px.at[x], px.at[x], ps.at[d], pr.at[d], z * NX + xx) for d, xx in enumerate(cross)
    ]
    for copy in p_cross:
        copy.start()

    v_pair.wait()
    v_cross2 = cross_copies(vg, 1 - head, 1)
    for copy in v_cross2:
        copy.start()
    row, col = iotas((HD, HD))
    for a in range(2):
        for b in range(2):
            rows = slice(b * HD, (b + 1) * HD)
            for src, dst in ((q, qlocal), (k, klocal)):
                part = src[rows, a * HD : (a + 1) * HD].astype(F32)
                coef = jnp.where(row >= col, nt3(part, units[a, rows]), 0.0)
                dst[a, rows] = part - nn3(coef, updates[a, rows])

    for copy in p_cross:
        copy.wait()
    for a in range(2):
        one = px[0, a]
        two = nn3(one, px[1, a])
        tz[z, a] = nn3(two, nn3(px[2, a], px[3, a]))
        three = nn3(two, px[2, a])
        totals[a] = jnp.where(
            x == 0, identity(), jnp.where(x == 1, one, jnp.where(x == 2, two, three))
        )
    band = pl.ds(pl.multiple_of(x * 32, 32), 32)

    def t_copy(to, source):
        return send(
            tz.at[source, :, band], tz.at[source, :, band], ts.at[to], tr.at[source], to * NX + x
        )

    def t_forward(source):
        return [
            send(
                tz.at[source, :, band],
                tz.at[source, :, band],
                fs.at[source, d],
                fr.at[source, d],
                z * NX + xx,
            )
            for d, xx in enumerate(cross)
        ]

    def t_start(to, carry):
        t_copy(to, z).start()
        return carry

    lax.fori_loop(z + 1, NZ, t_start, 0)

    def t_step(d, carry):
        @pl.when(d <= z)
        def _():
            t_copy(z, z - d).wait_recv()
            for copy in t_forward(z - d):
                copy.start()

        @pl.when(d > 2)
        def _():
            source = z - d + 2
            for copy in t_forward(source):
                copy.wait()
            for a in range(2):
                totals[a] = nn3(tz[source, a], totals[a])

        return carry

    lax.fori_loop(1, jnp.where(z > 0, z + 3, 1), t_step, 0)
    for a in range(2):
        prefixes[a, 0] = totals[a]
        prefixes[a, 1] = nn3(totals[a], products[a, 0])
        for b in range(2):
            rows = slice(b * HD, (b + 1) * HD)
            ks[a, rows] = nt3(klocal[a, rows], prefixes[a, b]).astype(BF)
    k_pair = pair_copy(ks, kg, 1)
    k_pair.start()
    kg[head, rows_at(x)] = ks[head]
    k_cross = cross_copies(kg, head, 2)
    for copy in k_cross:
        copy.start()
    for a in range(2):
        for b in range(2):
            rows = slice(b * HD, (b + 1) * HD)
            qs[a, rows] = nt3(qlocal[a, rows], prefixes[a, b]).astype(BF)
    line_start(qs, qg, 1)
    qg[z] = qs[head]
    k_pair.wait()
    k_cross2 = cross_copies(kg, 1 - head, 3)
    for copy in k_cross2:
        copy.start()

    def t_done(to, carry):
        t_copy(to, z).wait_send()
        return carry

    lax.fori_loop(z + 1, NZ, t_done, 0)
    for copy in v_cross + v_cross2 + k_cross + k_cross2:
        copy.wait()

    top, total, delta = (held.at[z % 4, i] for i in range(3))
    top[...] = jnp.full(top.shape, LOW, F32)
    total[...] = jnp.zeros(total.shape, F32)
    delta[...] = jnp.zeros(delta.shape, F32)
    key_at, query_at = iotas((ROWS, ROWS))

    def join(at, peak, weight, moment):
        old = top[at, :]
        new = jnp.maximum(old, peak)
        keep, take = jnp.exp2(old - new), jnp.exp2(peak - new)
        top[at, :] = new
        total[at, :] = total[at, :] * keep + weight * take
        delta[at, :] = delta[at, :] * keep + moment * take

    def forward_full(r, slot):
        query, cot = qg[r], cg[r]
        peak = None
        for j in range(NX):
            rows = slice(j * ROWS, (j + 1) * ROWS)
            score = nt(kg[slot, rows], query) * SCALE2
            s_scr[rows] = score
            high = jnp.max(score, axis=0, keepdims=True)
            peak = high if peak is None else jnp.maximum(peak, high)
        weight = moment = jnp.zeros((1, ROWS), F32)
        for j in range(NX):
            rows = slice(j * ROWS, (j + 1) * ROWS)
            p = jnp.exp2(s_scr[rows] - peak)
            weight = weight + jnp.sum(p, axis=0, keepdims=True)
            moment = moment + jnp.sum(p * nt(vg[slot, rows], cot), axis=0, keepdims=True)
        join(pl.ds(r, 1), peak, weight, moment)

    def forward_edge(r, slot):
        def step(j, carry):
            rows = rows_at(j)
            live = key_at + j * ROWS <= query_at + x * ROWS
            score = jnp.where(live, nt(kg[slot, rows], qg[r]) * SCALE2, LOW)
            peak = jnp.max(score, axis=0, keepdims=True)
            p = jnp.where(live, jnp.exp2(score - peak), 0.0)
            moment = jnp.sum(p * nt(vg[slot, rows], cg[r]), axis=0, keepdims=True)
            join(pl.ds(r, 1), peak, jnp.sum(p, axis=0, keepdims=True), moment)
            return carry

        lax.fori_loop(0, x + 1, step, 0)

    def forward_row(n, carry):
        offset = (n + 1) // 2
        r = (z + NZ + jnp.where(n % 2 == 1, offset, -offset)) % NZ

        @pl.when((r != z) & (r >= low_row))
        def _():
            line_copy(cs, cg, 0, z, r).wait_recv()
            line_copy(qs, qg, 1, z, r).wait_recv()

        def slot_step(slot, carry):
            key_row = jnp.where(slot == 0, low_row, NZ - 1 - low_row)

            @pl.when(r > key_row)
            def _():
                forward_full(r, slot)

            @pl.when(r == key_row)
            def _():
                forward_edge(r, slot)

            return carry

        return lax.fori_loop(0, 2, slot_step, carry)

    lax.fori_loop(0, NZ, forward_row, 0)

    half_peers = [(head * 4 + (z + d) % 4) * NX + x for d in range(1, 4)]
    stat_copies = [
        send(held.at[z % 4], held.at[z % 4], ss.at[d], sr.at[d], peer)
        for d, peer in enumerate(half_peers)
    ]
    for copy in stat_copies:
        copy.start()
    line_wait_send(cs, cg, 0)
    line_wait_send(qs, qg, 1)
    dq_acc[...] = jnp.zeros(dq_acc.shape, F32)
    dk_acc[...] = jnp.zeros(dk_acc.shape, F32)
    dv_acc[...] = jnp.zeros(dv_acc.shape, F32)
    for slot in range(2):
        for j in range(NX):
            kt[slot, j] = kg[slot, j * ROWS : (j + 1) * ROWS].T
    for copy in stat_copies:
        copy.wait()
    peak = held[0, 0]
    for i in range(1, 4):
        peak = jnp.maximum(peak, held[i, 0])
    weight = moment = jnp.zeros(peak.shape, F32)
    for i in range(4):
        take = jnp.exp2(held[i, 0] - peak)
        weight = weight + held[i, 1] * take
        moment = moment + held[i, 2] * take
    log_total[...] = peak + jnp.log2(weight)
    delta_row[...] = moment / weight

    def tile(r, slot, j, rows, live):
        key, query, cot = kg[slot, rows], qg[r], cg[r]
        at = pl.ds(r, 1)
        score = nt(key, query) * SCALE2 - log_total[at, :]
        if live is not None:
            score = jnp.where(live, score, LOW)
        p = jnp.exp2(score)
        grad = (p * (nt(vg[slot, rows], cot) - delta_row[at, :])).astype(BF)
        dv_acc[slot, rows] += nn(p.astype(BF), cot)
        dk_acc[slot, rows] += nn(grad, query)
        return nn(kt[slot, j], grad)

    def backward_full(r, slot):
        total = None
        for j in range(NX):
            part = tile(r, slot, j, slice(j * ROWS, (j + 1) * ROWS), None)
            total = part if total is None else total + part
        dq_acc[r] += total

    def backward_edge(r, slot):
        def step(j, carry):
            live = key_at + j * ROWS <= query_at + x * ROWS
            dq_acc[r] += tile(r, slot, j, rows_at(j), live)
            return carry

        lax.fori_loop(0, x + 1, step, 0)

    def dq_copy(to, source):
        return send(dqt.at[to], rq.at[source], zs.at[2, to], zr.at[2, source], to * NX + x)

    def backward_row(n, carry):
        slot = jnp.where(n < NZ, 1 - head, head)
        key_row = jnp.where(slot == 0, low_row, NZ - 1 - low_row)
        m = n % NZ
        offset = 4 - (m + 1) // 2
        r = (z + NZ + jnp.where(m % 2 == 1, offset, -offset)) % NZ

        @pl.when(r > key_row)
        def _():
            backward_full(r, slot)

        @pl.when(r == key_row)
        def _():
            backward_edge(r, slot)

        @pl.when((n >= NZ) & (r >= low_row))
        def _():
            dqt[r] = (dq_acc[r] * SCALE).astype(BF)

            @pl.when(r != z)
            def _():
                dq_copy(r, z).start()

        @pl.when((n == NZ - 1) | (n == 2 * NZ - 1))
        def _():
            i = n // NZ
            dkv[slot, :, :HD] = (dk_acc[slot] * SCALE).astype(BF)
            dkv[slot, :, HD:] = dv_acc[slot].astype(BF)
            rx[x, i] = dkv[slot, rows_at(x)]
            for copy in kv_copies(i):
                copy.start()

        return carry

    def kv_copies(i):
        slot = jnp.where(i == 0, 1 - head, head)
        return [
            send(dkv.at[slot, rows_at(xx)], rx.at[x, i], xs.at[4 + i, d], xr.at[4 + i, d], z * NX + xx)
            for d, xx in enumerate(cross)
        ]

    lax.fori_loop(0, 2 * NZ, backward_row, 0)

    def summed(i):
        return (rx[0, i].astype(F32) + rx[1, i].astype(F32)) + (
            rx[2, i].astype(F32) + rx[3, i].astype(F32)
        )

    for copy in kv_copies(0):
        copy.wait()
    pair_out[0] = summed(0).astype(BF)
    pair = send(pair_out.at[0], pair_out.at[1], os.at[2], orr.at[2], other * NX + x)
    pair.start()

    rq[z] = dqt[z]

    def dq_wait(d, carry):
        to = (z + d) % NZ

        @pl.when(to >= low_row)
        def _():
            dq_copy(to, z).wait_send()

        @pl.when(z >= jnp.minimum(to, NZ - 1 - to))
        def _():
            dq_copy(z, to).wait_recv()

        @pl.when(z < jnp.minimum(to, NZ - 1 - to))
        def _():
            rq[to] = jnp.zeros(rq.shape[1:], BF)

        return carry

    lax.fori_loop(1, NZ, dq_wait, 0)

    def turn_back(i, a, b, part):
        rows, cols = slice(b * HD, (b + 1) * HD), slice(a * HD, (a + 1) * HD)
        back = nn3(part, prefixes[a, b])
        coef = jnp.where(row >= col, nt3(back, updates[a, rows]), 0.0)
        grads[i, rows, cols] = (back - nn3(coef, units[a, rows])).astype(BF)

    for a in range(2):
        total = rq[4 * a].astype(F32)
        for i in range(1, 4):
            total = total + rq[4 * a + i].astype(F32)
        total = total.T
        for b in range(2):
            turn_back(0, a, b, total[b * HD : (b + 1) * HD])
    for copy in kv_copies(1):
        copy.wait()
    kv[head] = summed(1)
    pair.wait()
    kv[1 - head] = pair_out[1].astype(F32)
    for a in range(2):
        grads[2, :, a * HD : (a + 1) * HD] = kv[a, :, HD:].astype(BF)
        for b in range(2):
            turn_back(1, a, b, kv[a, b * HD : (b + 1) * HD, :HD])
    for load in loads:
        load.wait()

    def columns(block):
        at = pl.ds(pl.multiple_of(block * 512, 512), 512)
        return (
            nt(grads[0], w[0, at, :]) + nt(grads[1], w[1, at, :]) + nt(grads[2], w[2, at, :])
        )

    blocks = order + [y]
    swaps, hops = [], []

    def give(i):
        mine[i] = columns(blocks[i] * 2 + 1 - core).astype(BF)
        swap = send(mine.at[i], theirs.at[i], ms.at[i], mr.at[i], mate, "head")
        swap.start()
        swaps.append(swap)

    give(0)
    give(1)
    for i, yy in enumerate(blocks):
        part = columns(yy * 2 + core)
        if i + 2 < 4:
            give(i + 2)
        swaps[i].wait()
        part = part + theirs[i].astype(F32)
        if i < 3:
            relay[i] = part.astype(BF)
            hop = send(relay.at[i], landed.at[i], ys.at[i], yr.at[i], yy * 2 + core, "head")
            hop.start()
            hops.append(hop)
        else:
            out[...] = part
    for hop in hops:
        hop.wait()
    out[...] = (out[...] + landed[0].astype(F32)) + (
        landed[1].astype(F32) + landed[2].astype(F32)
    )


def on_device(query, key, value, householder, cotangent, w_query, w_key, w_value):
    dma = pltpu.SemaphoreType.DMA
    own, own32 = ((2, ROWS, HD), BF), ((2, ROWS, HD), F32)
    lines, keys = ((NZ, ROWS, HD), BF), ((2, NX * ROWS, HD), BF)
    square = (HD, HD)
    stat = ((NZ, ROWS), F32)
    acc = ((2, NX * ROWS, HD), F32)
    block = (ROWS, 2 * HD)
    wide = (ROWS, 512)
    scratch = [
        lines, lines, keys, keys, own32, own32, ((2, 2) + square, F32),
        own, own, own, own, ((NX, 2) + square, F32), ((NZ, 2) + square, F32), own32, own32,
        ((2, 2) + square, F32), ((4,) + square, F32), ((4,) + square, F32), ((2,) + square, F32),
        ((NX * ROWS, ROWS), F32), ((4, 3, NZ, ROWS), F32), stat, stat,
        ((2, NX, HD, ROWS), BF), ((NZ, HD, ROWS), F32), acc, acc,
        ((NZ, HD, ROWS), BF), ((2, NX * ROWS, 2 * HD), BF), ((NZ, HD, ROWS), BF),
        ((NX, 2) + block, BF), ((2,) + block, BF), ((2,) + block, F32),
        ((3, 4096, ROWS), BF), ((3,) + block, BF),
        ((4,) + wide, BF), ((4,) + wide, BF), ((3,) + wide, BF), ((3,) + wide, BF),
    ]
    sems = [
        (3, 8), (3, 8), (6, 3), (6, 3), (3,), (3,), (8,), (8,), (8, 3), (8, 3), (3,), (3,),
        (3,), (3,), (3,), (4,), (4,), (3,), (3,),
    ]
    vmem = pl.BlockSpec(memory_space=pltpu.VMEM)
    return pl.pallas_call(
        whole_kernel,
        out_shape=jax.ShapeDtypeStruct(wide, F32),
        in_specs=[vmem] * 5 + [pl.BlockSpec(memory_space=pl.ANY)] * 3,
        out_specs=vmem,
        scratch_shapes=[pltpu.VMEM(*s) for s in scratch] + [dma(s) for s in sems],
        compiler_params=pltpu.CompilerParams(
            vmem_limit_bytes=VMEM_BYTES, collective_id=0, has_side_effects=True
        ),
    )(householder, query, key, value, cotangent, w_query, w_key, w_value)


def solution(mesh):
    return jax.shard_map(
        on_device,
        mesh=mesh,
        in_specs=(P("ctx", "head"),) * 5 + (P(None, "head"),) * 3,
        out_specs=P("ctx", "head"),
        check_vma=False,
    )
```

```python
import math

import jax
import jax.numpy as jnp
from jax import lax
from jax.experimental import pallas as pl
from jax.experimental.pallas import tpu as pltpu
from jax.sharding import PartitionSpec as P

MESH = pl.DeviceIdType.MESH
BF = jnp.bfloat16
F32 = jnp.float32
ROWS = 256
HD = 128
NZ, NX = 8, 4
SCALE = HD**-0.5
SCALE2 = SCALE * math.log2(math.e)
VMEM_BYTES = 56 * 1024 * 1024
LOW = -1e30


def nn(a, b):
    return lax.dot_general(a, b, (((1,), (0,)), ((), ())), preferred_element_type=F32)


def nt(a, b):
    return lax.dot_general(a, b, (((1,), (1,)), ((), ())), preferred_element_type=F32)


def split(a):
    high = a.astype(BF)
    return high, (a - high.astype(F32)).astype(BF)


def nn3(a, b):
    ah, al = split(a)
    bh, bl = split(b)
    return nn(ah, bh) + (nn(al, bh) + nn(ah, bl))


def nt3(a, b):
    ah, al = split(a)
    bh, bl = split(b)
    return nt(ah, bh) + (nt(al, bh) + nt(ah, bl))


def nn2(a, b):
    bh, bl = split(b)
    return nn(a, bh) + nn(a, bl)


def iotas(shape):
    return lax.broadcasted_iota(jnp.int32, shape, 0), lax.broadcasted_iota(jnp.int32, shape, 1)


def identity():
    row, col = iotas((HD, HD))
    return jnp.where(row == col, 1.0, 0.0).astype(F32)


def place():
    me = lax.axis_index("ctx")
    return me // NX, me % NX


def send(src, dst, send_sem, recv_sem, peer, axis="ctx"):
    return pltpu.make_async_remote_copy(
        src_ref=src,
        dst_ref=dst,
        send_sem=send_sem,
        recv_sem=recv_sem,
        device_id={axis: peer},
        device_id_type=MESH,
    )


def reflectors(hh, units, updates, products, lowers, inverses):
    row, col = iotas((HD, HD))
    chunks = [(a, b, slice(b * HD, (b + 1) * HD)) for a in range(2) for b in range(2)]
    for i, (a, b, rows) in enumerate(chunks):
        vec = hh[rows, a * HD : (a + 1) * HD].astype(F32)
        unit = vec * lax.rsqrt(jnp.sum(vec * vec, axis=1, keepdims=True) + 1e-6)
        lower = 2.0 * jnp.where(row > col, nt3(unit, unit), 0.0)
        units[a, rows] = unit
        lowers[i] = lower
        inverses[i] = identity() - jnp.where(row // 2 == col // 2, lower, 0.0)

    def join(level, carry):
        row_part, col_part = lax.shift_right_logical(row, level), lax.shift_right_logical(col, level)
        pick = (row_part == col_part + 1) & ((col_part & 1) == 0)
        for i in range(4):
            inverse = inverses[i]
            inner = nn3(jnp.where(pick, lowers[i], 0.0), inverse)
            inverses[i] = inverse - nn3(inverse, inner)
        return carry

    lax.fori_loop(1, 7, join, 0)
    for i, (a, b, rows) in enumerate(chunks):
        unit, inverse = units[a, rows], inverses[i]
        updates[a, rows] = 2.0 * nn3(inverse, unit)
        turned = 2.0 * nt3(unit.T, inverse)
        products[a, b] = identity() - nn3(turned, unit)


def rows_at(block):
    return pl.ds(pl.multiple_of(block * ROWS, ROWS), ROWS)


def whole_kernel(
    hh_in, q_in, k_in, v_in, c_in, wq, wk, wv,
    out,
    hh, q, k, v, c, qg, cg, kg, vg, units, updates, prefixes,
    qs, ks, cs, vs, px, tz, qlocal, klocal, products, lowers, inverses, totals,
    s_scr, held, log_total, delta_row,
    kt, dq_acc, dk_acc, dv_acc, dqt, dkv, rq, rx, pair_out, kv,
    w, grads, mine, theirs, relay, landed, joined,
    zs, zr, xs, xr, ps, pr, ts, tr, fs, fr, os, orr, ss, sr, ws, ins, ms, mr, ys, yr,
):
    z, x = place()
    me = lax.axis_index("head")
    y, core = me // 2, me % 2
    mate = y * 2 + 1 - core
    head = z // 4
    low_row = jnp.minimum(z, NZ - 1 - z)
    other = NZ - 1 - z
    line = [(z + d) % NZ for d in range(1, NZ)]
    cross = [(x + d) % NX for d in range(1, NX)]
    above, below = (y + 1) % 4, (y + 3) % 4
    pairs = ((c_in, c), (v_in, v), (hh_in, hh), (q_in, q), (k_in, k))
    reads = [pltpu.make_async_copy(src, dst, ins.at[i]) for i, (src, dst) in enumerate(pairs)]
    for read in reads:
        read.start()
    barrier = pltpu.get_barrier_semaphore()
    peers = [{"ctx": zz * NX + x} for zz in line] + [{"ctx": z * NX + xx} for xx in cross]
    peers = peers + [{"head": mate}] + [{"head": yy * 2 + core} for yy in (above, below)]
    for peer in peers:
        pl.semaphore_signal(barrier, inc=1, device_id=peer, device_id_type=MESH)
    pl.semaphore_wait(barrier, len(peers))

    def line_copy(src, dst, i, to, source):
        return send(src.at[to // 4], dst.at[source], zs.at[i, to], zr.at[i, source], to * NX + x)

    def line_start(src, dst, i):
        def step(d, carry):
            to = (z + d) % NZ

            @pl.when(z >= jnp.minimum(to, NZ - 1 - to))
            def _():
                line_copy(src, dst, i, to, z).start()

            return carry

        lax.fori_loop(1, NZ, step, 0)

    def line_wait_send(src, dst, i):
        def step(d, carry):
            to = (z + d) % NZ

            @pl.when(z >= jnp.minimum(to, NZ - 1 - to))
            def _():
                line_copy(src, dst, i, to, z).wait_send()

            return carry

        lax.fori_loop(1, NZ, step, 0)

    def pair_copy(src, dst, i):
        return send(
            src.at[1 - head], dst.at[head, rows_at(x)], os.at[i], orr.at[i], other * NX + x
        )

    def cross_copies(dst, slot, i):
        return [
            send(dst.at[slot, rows_at(x)], dst.at[slot, rows_at(x)], xs.at[i, d], xr.at[i, d], z * NX + xx)
            for d, xx in enumerate(cross)
        ]

    for read in reads:
        read.wait()
    for part in range(2):
        cols = slice(part * HD, (part + 1) * HD)
        cs[part] = c[:, cols]
        vs[part] = v[:, cols]
    v_pair = pair_copy(vs, vg, 0)
    v_pair.start()
    line_start(cs, cg, 0)
    cg[z] = cs[head]
    vg[head, rows_at(x)] = vs[head]
    v_cross = cross_copies(vg, head, 0)
    for copy in v_cross:
        copy.start()
    loads = [pltpu.make_async_copy(src, w.at[i], ws.at[i]) for i, src in enumerate((wq, wk, wv))]
    for load in loads:
        load.start()

    reflectors(hh, units, updates, products, lowers, inverses)
    for a in range(2):
        px[x, a] = nn3(products[a, 0], products[a, 1])
    p_cross = [
        send(px.at[x], px.at[x], ps.at[d], pr.at[d], z * NX + xx) for d, xx in enumerate(cross)
    ]
    for copy in p_cross:
        copy.start()

    v_pair.wait()
    v_cross2 = cross_copies(vg, 1 - head, 1)
    for copy in v_cross2:
        copy.start()
    row, col = iotas((HD, HD))
    for a in range(2):
        for b in range(2):
            rows = slice(b * HD, (b + 1) * HD)
            for src, dst in ((q, qlocal), (k, klocal)):
                part = src[rows, a * HD : (a + 1) * HD].astype(F32)
                coef = jnp.where(row >= col, nt3(part, units[a, rows]), 0.0)
                dst[a, rows] = part - nn3(coef, updates[a, rows])

    for copy in p_cross:
        copy.wait()
    for a in range(2):
        one = px[0, a]
        two = nn3(one, px[1, a])
        tz[z, a] = nn3(two, nn3(px[2, a], px[3, a])).astype(BF)
        three = nn3(two, px[2, a])
        totals[a] = jnp.where(
            x == 0, identity(), jnp.where(x == 1, one, jnp.where(x == 2, two, three))
        )
    band = pl.ds(pl.multiple_of(x * 32, 32), 32)

    def t_copy(to, source):
        return send(
            tz.at[source, :, band], tz.at[source, :, band], ts.at[to], tr.at[source], to * NX + x
        )

    def t_forward(source):
        return [
            send(
                tz.at[source, :, band],
                tz.at[source, :, band],
                fs.at[source, d],
                fr.at[source, d],
                z * NX + xx,
            )
            for d, xx in enumerate(cross)
        ]

    def t_start(to, carry):
        t_copy(to, z).start()
        return carry

    lax.fori_loop(z + 1, NZ, t_start, 0)

    def t_step(d, carry):
        @pl.when(d <= z)
        def _():
            t_copy(z, z - d).wait_recv()
            for copy in t_forward(z - d):
                copy.start()

        @pl.when(d > 2)
        def _():
            source = z - d + 2
            for copy in t_forward(source):
                copy.wait()
            for a in range(2):
                totals[a] = nn2(tz[source, a], totals[a])

        return carry

    lax.fori_loop(1, jnp.where(z > 0, z + 3, 1), t_step, 0)
    for a in range(2):
        prefixes[a, 0] = totals[a]
        prefixes[a, 1] = nn3(totals[a], products[a, 0])
        for b in range(2):
            rows = slice(b * HD, (b + 1) * HD)
            ks[a, rows] = nt3(klocal[a, rows], prefixes[a, b]).astype(BF)
    k_pair = pair_copy(ks, kg, 1)
    k_pair.start()
    kg[head, rows_at(x)] = ks[head]
    k_cross = cross_copies(kg, head, 2)
    for copy in k_cross:
        copy.start()
    for a in range(2):
        for b in range(2):
            rows = slice(b * HD, (b + 1) * HD)
            qs[a, rows] = nt3(qlocal[a, rows], prefixes[a, b]).astype(BF)
    line_start(qs, qg, 1)
    qg[z] = qs[head]
    k_pair.wait()
    k_cross2 = cross_copies(kg, 1 - head, 3)
    for copy in k_cross2:
        copy.start()

    def t_done(to, carry):
        t_copy(to, z).wait_send()
        return carry

    lax.fori_loop(z + 1, NZ, t_done, 0)
    for copy in v_cross + v_cross2 + k_cross:
        copy.wait()

    top, total, delta = (held.at[z % 4, i] for i in range(3))
    top[...] = jnp.full(top.shape, LOW, F32)
    total[...] = jnp.zeros(total.shape, F32)
    delta[...] = jnp.zeros(delta.shape, F32)
    key_at, query_at = iotas((ROWS, ROWS))

    def join(at, peak, weight, moment):
        old = top[at, :]
        new = jnp.maximum(old, peak)
        keep, take = jnp.exp2(old - new), jnp.exp2(peak - new)
        top[at, :] = new
        total[at, :] = total[at, :] * keep + weight * take
        delta[at, :] = delta[at, :] * keep + moment * take

    def forward_full(r, slot):
        query, cot = qg[r], cg[r]
        peak = None
        for j in range(NX):
            rows = slice(j * ROWS, (j + 1) * ROWS)
            score = nt(kg[slot, rows], query) * SCALE2
            s_scr[rows] = score
            high = jnp.max(score, axis=0, keepdims=True)
            peak = high if peak is None else jnp.maximum(peak, high)
        weight = moment = jnp.zeros((1, ROWS), F32)
        for j in range(NX):
            rows = slice(j * ROWS, (j + 1) * ROWS)
            p = jnp.exp2(s_scr[rows] - peak)
            weight = weight + jnp.sum(p, axis=0, keepdims=True)
            moment = moment + jnp.sum(p * nt(vg[slot, rows], cot), axis=0, keepdims=True)
        join(pl.ds(r, 1), peak, weight, moment)

    def forward_edge(r, slot):
        def step(j, carry):
            rows = rows_at(j)
            live = key_at + j * ROWS <= query_at + x * ROWS
            score = jnp.where(live, nt(kg[slot, rows], qg[r]) * SCALE2, LOW)
            peak = jnp.max(score, axis=0, keepdims=True)
            p = jnp.where(live, jnp.exp2(score - peak), 0.0)
            moment = jnp.sum(p * nt(vg[slot, rows], cg[r]), axis=0, keepdims=True)
            join(pl.ds(r, 1), peak, jnp.sum(p, axis=0, keepdims=True), moment)
            return carry

        lax.fori_loop(0, x + 1, step, 0)

    def forward_row(n, carry):
        slot = jnp.where(n < NZ, head, 1 - head)
        key_row = jnp.where(slot == 0, low_row, NZ - 1 - low_row)
        m = n % NZ
        offset = (m + 1) // 2
        r = (z + NZ + jnp.where(m % 2 == 1, offset, -offset)) % NZ

        @pl.when((n < NZ) & (r != z) & (r >= low_row))
        def _():
            line_copy(cs, cg, 0, z, r).wait_recv()
            line_copy(qs, qg, 1, z, r).wait_recv()

        @pl.when(n == NZ)
        def _():
            for copy in k_cross2:
                copy.wait()

        @pl.when(r > key_row)
        def _():
            forward_full(r, slot)

        @pl.when(r == key_row)
        def _():
            forward_edge(r, slot)

        return carry

    lax.fori_loop(0, 2 * NZ, forward_row, 0)

    half_peers = [(head * 4 + (z + d) % 4) * NX + x for d in range(1, 4)]
    stat_copies = [
        send(held.at[z % 4], held.at[z % 4], ss.at[d], sr.at[d], peer)
        for d, peer in enumerate(half_peers)
    ]
    for copy in stat_copies:
        copy.start()
    line_wait_send(cs, cg, 0)
    line_wait_send(qs, qg, 1)
    dq_acc[...] = jnp.zeros(dq_acc.shape, F32)
    dk_acc[...] = jnp.zeros(dk_acc.shape, F32)
    dv_acc[...] = jnp.zeros(dv_acc.shape, F32)
    for slot in range(2):
        for j in range(NX):
            kt[slot, j] = kg[slot, j * ROWS : (j + 1) * ROWS].T
    for copy in stat_copies:
        copy.wait()
    peak = held[0, 0]
    for i in range(1, 4):
        peak = jnp.maximum(peak, held[i, 0])
    weight = moment = jnp.zeros(peak.shape, F32)
    for i in range(4):
        take = jnp.exp2(held[i, 0] - peak)
        weight = weight + held[i, 1] * take
        moment = moment + held[i, 2] * take
    log_total[...] = peak + jnp.log2(weight)
    delta_row[...] = moment / weight

    def tile(r, slot, j, rows, live):
        key, query, cot = kg[slot, rows], qg[r], cg[r]
        at = pl.ds(r, 1)
        score = nt(key, query) * SCALE2 - log_total[at, :]
        if live is not None:
            score = jnp.where(live, score, LOW)
        p = jnp.exp2(score)
        grad = (p * (nt(vg[slot, rows], cot) - delta_row[at, :])).astype(BF)
        dv_acc[slot, rows] += nn(p.astype(BF), cot)
        dk_acc[slot, rows] += nn(grad, query)
        return nn(kt[slot, j], grad)

    def backward_full(r, slot):
        total = None
        for j in range(NX):
            part = tile(r, slot, j, slice(j * ROWS, (j + 1) * ROWS), None)
            total = part if total is None else total + part
        dq_acc[r] += total

    def backward_edge(r, slot):
        def step(j, carry):
            live = key_at + j * ROWS <= query_at + x * ROWS
            dq_acc[r] += tile(r, slot, j, rows_at(j), live)
            return carry

        lax.fori_loop(0, x + 1, step, 0)

    def dq_copy(to, source):
        return send(dqt.at[to], rq.at[source], zs.at[2, to], zr.at[2, source], to * NX + x)

    def backward_row(n, carry):
        slot = jnp.where(n < NZ, 1 - head, head)
        key_row = jnp.where(slot == 0, low_row, NZ - 1 - low_row)
        m = n % NZ
        offset = 4 - (m + 1) // 2
        r = (z + NZ + jnp.where(m % 2 == 1, offset, -offset)) % NZ

        @pl.when(r > key_row)
        def _():
            backward_full(r, slot)

        @pl.when(r == key_row)
        def _():
            backward_edge(r, slot)

        @pl.when((n >= NZ) & (r >= low_row))
        def _():
            dqt[r] = (dq_acc[r] * SCALE).astype(BF)

            @pl.when(r != z)
            def _():
                dq_copy(r, z).start()

        @pl.when((n == NZ - 1) | (n == 2 * NZ - 1))
        def _():
            i = n // NZ
            dkv[slot, :, :HD] = (dk_acc[slot] * SCALE).astype(BF)
            dkv[slot, :, HD:] = dv_acc[slot].astype(BF)
            rx[x, i] = dkv[slot, rows_at(x)]
            for copy in kv_copies(i):
                copy.start()

        return carry

    def kv_copies(i):
        slot = jnp.where(i == 0, 1 - head, head)
        return [
            send(dkv.at[slot, rows_at(xx)], rx.at[x, i], xs.at[4 + i, d], xr.at[4 + i, d], z * NX + xx)
            for d, xx in enumerate(cross)
        ]

    lax.fori_loop(0, 2 * NZ, backward_row, 0)

    def summed(i):
        return (rx[0, i].astype(F32) + rx[1, i].astype(F32)) + (
            rx[2, i].astype(F32) + rx[3, i].astype(F32)
        )

    for copy in kv_copies(0):
        copy.wait()
    pair_out[0] = summed(0).astype(BF)
    pair = send(pair_out.at[0], pair_out.at[1], os.at[2], orr.at[2], other * NX + x)
    pair.start()

    rq[z] = dqt[z]

    def dq_wait(d, carry):
        to = (z + d) % NZ

        @pl.when(to >= low_row)
        def _():
            dq_copy(to, z).wait_send()

        @pl.when(z >= jnp.minimum(to, NZ - 1 - to))
        def _():
            dq_copy(z, to).wait_recv()

        @pl.when(z < jnp.minimum(to, NZ - 1 - to))
        def _():
            rq[to] = jnp.zeros(rq.shape[1:], BF)

        return carry

    lax.fori_loop(1, NZ, dq_wait, 0)

    def turn_back(i, a, b, part):
        rows, cols = slice(b * HD, (b + 1) * HD), pl.ds(pl.multiple_of(a * HD, HD), HD)
        back = nn3(part, prefixes[a, b])
        coef = jnp.where(row >= col, nt3(back, updates[a, rows]), 0.0)
        grads[i, rows, cols] = (back - nn3(coef, units[a, rows])).astype(BF)

    for a in range(2):
        total = rq[4 * a].astype(F32)
        for i in range(1, 4):
            total = total + rq[4 * a + i].astype(F32)
        total = total.T
        for b in range(2):
            turn_back(0, a, b, total[b * HD : (b + 1) * HD])
    for copy in kv_copies(1):
        copy.wait()

    def finish(a):
        grads[2, :, pl.ds(pl.multiple_of(a * HD, HD), HD)] = kv[a, :, HD:].astype(BF)
        for b in range(2):
            turn_back(1, a, b, kv[a, b * HD : (b + 1) * HD, :HD])

    kv[head] = summed(1)
    finish(head)
    pair.wait()
    kv[1 - head] = pair_out[1].astype(F32)
    finish(1 - head)
    for load in loads:
        load.wait()

    def columns(block):
        at = pl.ds(pl.multiple_of(block * 512, 512), 512)
        return (
            nt(grads[0], w[0, at, :]) + nt(grads[1], w[1, at, :]) + nt(grads[2], w[2, at, :])
        )

    half = ROWS // 2
    blocks = [(y + 2) % 4, above, below, y]
    swaps = []

    def give(i):
        mine[i] = columns(blocks[i] * 2 + 1 - core).astype(BF)
        swap = send(mine.at[i], theirs.at[i], ms.at[i], mr.at[i], mate, "head")
        swap.start()
        swaps.append(swap)

    def take(i):
        part = columns(blocks[i] * 2 + core)
        swaps[i].wait()
        return part + theirs[i].astype(F32)

    def hop(i, src, dst, to):
        copy = send(src, dst, ys.at[i], yr.at[i], to * 2 + core, "head")
        copy.start()
        return copy

    give(0)
    give(1)
    relay[0] = take(0).astype(BF)
    up = hop(0, relay.at[0, :half], landed.at[0, :half], above)
    down = hop(1, relay.at[0, half:], landed.at[0, half:], below)
    give(2)
    part = take(1)
    joined[0] = part[:half]
    relay[1, half:] = part[half:].astype(BF)
    hops = [hop(2, relay.at[1, half:], landed.at[1, half:], above)]
    give(3)
    part = take(2)
    joined[1] = part[half:]
    relay[2, :half] = part[:half].astype(BF)
    hops.append(hop(3, relay.at[2, :half], landed.at[2, :half], below))
    up.wait()
    relay[1, :half] = (joined[0] + landed[0, :half].astype(F32)).astype(BF)
    hops.append(hop(4, relay.at[1, :half], landed.at[1, :half], above))
    down.wait()
    relay[2, half:] = (joined[1] + landed[0, half:].astype(F32)).astype(BF)
    hops.append(hop(5, relay.at[2, half:], landed.at[2, half:], below))
    out[...] = take(3)
    for copy in hops:
        copy.wait()
    out[...] = out[...] + (landed[1].astype(F32) + landed[2].astype(F32))


def on_device(query, key, value, householder, cotangent, w_query, w_key, w_value):
    dma = pltpu.SemaphoreType.DMA
    own, own32 = ((2, ROWS, HD), BF), ((2, ROWS, HD), F32)
    lines, keys = ((NZ, ROWS, HD), BF), ((2, NX * ROWS, HD), BF)
    square = (HD, HD)
    stat = ((NZ, ROWS), F32)
    acc = ((2, NX * ROWS, HD), F32)
    block = (ROWS, 2 * HD)
    wide = (ROWS, 512)
    scratch = [(block, BF)] * 5 + [
        lines, lines, keys, keys, own32, own32, ((2, 2) + square, F32),
        own, own, own, own, ((NX, 2) + square, F32), ((NZ, 2) + square, BF), own32, own32,
        ((2, 2) + square, F32), ((4,) + square, F32), ((4,) + square, F32), ((2,) + square, F32),
        ((NX * ROWS, ROWS), F32), ((4, 3, NZ, ROWS), F32), stat, stat,
        ((2, NX, HD, ROWS), BF), ((NZ, HD, ROWS), F32), acc, acc,
        ((NZ, HD, ROWS), BF), ((2, NX * ROWS, 2 * HD), BF), ((NZ, HD, ROWS), BF),
        ((NX, 2) + block, BF), ((2,) + block, BF), ((2,) + block, F32),
        ((3, 4096, ROWS), BF), ((3,) + block, BF),
        ((4,) + wide, BF), ((4,) + wide, BF), ((3,) + wide, BF), ((3,) + wide, BF),
        ((2, ROWS // 2, 512), F32),
    ]
    sems = [
        (3, 8), (3, 8), (6, 3), (6, 3), (3,), (3,), (8,), (8,), (8, 3), (8, 3), (3,), (3,),
        (3,), (3,), (3,), (5,), (4,), (4,), (6,), (6,),
    ]
    vmem = pl.BlockSpec(memory_space=pltpu.VMEM)
    return pl.pallas_call(
        whole_kernel,
        out_shape=jax.ShapeDtypeStruct(wide, F32),
        in_specs=[pl.BlockSpec(memory_space=pl.ANY)] * 8,
        out_specs=vmem,
        scratch_shapes=[pltpu.VMEM(*s) for s in scratch] + [dma(s) for s in sems],
        compiler_params=pltpu.CompilerParams(
            vmem_limit_bytes=VMEM_BYTES, collective_id=0, has_side_effects=True
        ),
    )(householder, query, key, value, cotangent, w_query, w_key, w_value)


def solution(mesh):
    return jax.shard_map(
        on_device,
        mesh=mesh,
        in_specs=(P("ctx", "head"),) * 5 + (P(None, "head"),) * 3,
        out_specs=P("ctx", "head"),
        check_vma=False,
    )
```

```python
import math

import jax
import jax.numpy as jnp
from jax import lax
from jax.experimental import pallas as pl
from jax.experimental.pallas import tpu as pltpu
from jax.sharding import PartitionSpec as P

MESH = pl.DeviceIdType.MESH
BF = jnp.bfloat16
F32 = jnp.float32
ROWS = 256
HD = 128
NZ, NX = 8, 4
SCALE = HD**-0.5
SCALE2 = SCALE * math.log2(math.e)
VMEM_BYTES = 56 * 1024 * 1024
LOW = -1e30


def nn(a, b):
    return lax.dot_general(a, b, (((1,), (0,)), ((), ())), preferred_element_type=F32)


def nt(a, b):
    return lax.dot_general(a, b, (((1,), (1,)), ((), ())), preferred_element_type=F32)


def split(a):
    high = a.astype(BF)
    return high, (a - high.astype(F32)).astype(BF)


def nn3(a, b):
    ah, al = split(a)
    bh, bl = split(b)
    return nn(ah, bh) + (nn(al, bh) + nn(ah, bl))


def nt3(a, b):
    ah, al = split(a)
    bh, bl = split(b)
    return nt(ah, bh) + (nt(al, bh) + nt(ah, bl))


def nn2(a, b):
    bh, bl = split(b)
    return nn(a, bh) + nn(a, bl)


def iotas(shape):
    return lax.broadcasted_iota(jnp.int32, shape, 0), lax.broadcasted_iota(jnp.int32, shape, 1)


def identity():
    row, col = iotas((HD, HD))
    return jnp.where(row == col, 1.0, 0.0).astype(F32)


def place():
    me = lax.axis_index("ctx")
    return me // NX, me % NX


def send(src, dst, send_sem, recv_sem, peer, axis="ctx"):
    return pltpu.make_async_remote_copy(
        src_ref=src,
        dst_ref=dst,
        send_sem=send_sem,
        recv_sem=recv_sem,
        device_id={axis: peer},
        device_id_type=MESH,
    )


def reflectors(hh, units, updates, products, lowers, inverses):
    row, col = iotas((HD, HD))
    chunks = [(a, b, slice(b * HD, (b + 1) * HD)) for a in range(2) for b in range(2)]
    for i, (a, b, rows) in enumerate(chunks):
        vec = hh[rows, a * HD : (a + 1) * HD].astype(F32)
        unit = vec * lax.rsqrt(jnp.sum(vec * vec, axis=1, keepdims=True) + 1e-6)
        lower = 2.0 * jnp.where(row > col, nt3(unit, unit), 0.0)
        units[a, rows] = unit
        lowers[i] = lower
        inverses[i] = identity() - jnp.where(row // 2 == col // 2, lower, 0.0)

    def join(level, carry):
        row_part, col_part = lax.shift_right_logical(row, level), lax.shift_right_logical(col, level)
        pick = (row_part == col_part + 1) & ((col_part & 1) == 0)
        for i in range(4):
            inverse = inverses[i]
            inner = nn3(jnp.where(pick, lowers[i], 0.0), inverse)
            inverses[i] = inverse - nn3(inverse, inner)
        return carry

    lax.fori_loop(1, 7, join, 0)
    for i, (a, b, rows) in enumerate(chunks):
        unit, inverse = units[a, rows], inverses[i]
        updates[a, rows] = 2.0 * nn3(inverse, unit)
        turned = 2.0 * nt3(unit.T, inverse)
        products[a, b] = identity() - nn3(turned, unit)


def rows_at(block):
    return pl.ds(pl.multiple_of(block * ROWS, ROWS), ROWS)


def whole_kernel(
    hh_in, q_in, k_in, v_in, c_in, wq, wk, wv,
    out,
    hh, q, k, v, c, qg, cg, kg, vg, units, updates, prefixes,
    qs, ks, cs, vs, px, tz, qlocal, klocal, products, lowers, inverses, totals,
    gw, pt, peaks, held, log_total, delta_row,
    kt, dq_acc, dk_acc, dv_acc, dqt, dkv, rq, rx, pair_out, kv,
    w, grads, mine, theirs, relay, landed, joined,
    zs, zr, xs, xr, ps, pr, ts, tr, fs, fr, os, orr, ss, sr, ws, ins, ms, mr, ys, yr,
):
    z, x = place()
    me = lax.axis_index("head")
    y, core = me // 2, me % 2
    mate = y * 2 + 1 - core
    head = z // 4
    low_row = jnp.minimum(z, NZ - 1 - z)
    other = NZ - 1 - z
    line = [(z + d) % NZ for d in range(1, NZ)]
    cross = [(x + d) % NX for d in range(1, NX)]
    above, below = (y + 1) % 4, (y + 3) % 4
    pairs = ((c_in, c), (v_in, v), (hh_in, hh), (q_in, q), (k_in, k))
    reads = [pltpu.make_async_copy(src, dst, ins.at[i]) for i, (src, dst) in enumerate(pairs)]
    for read in reads:
        read.start()
    barrier = pltpu.get_barrier_semaphore()
    peers = [{"ctx": zz * NX + x} for zz in line] + [{"ctx": z * NX + xx} for xx in cross]
    peers = peers + [{"head": mate}] + [{"head": yy * 2 + core} for yy in (above, below)]
    for peer in peers:
        pl.semaphore_signal(barrier, inc=1, device_id=peer, device_id_type=MESH)
    pl.semaphore_wait(barrier, len(peers))

    def line_copy(src, dst, i, to, source):
        return send(src.at[to // 4], dst.at[source], zs.at[i, to], zr.at[i, source], to * NX + x)

    def line_start(src, dst, i):
        def step(d, carry):
            to = (z + d) % NZ

            @pl.when(z >= jnp.minimum(to, NZ - 1 - to))
            def _():
                line_copy(src, dst, i, to, z).start()

            return carry

        lax.fori_loop(1, NZ, step, 0)

    def line_wait_send(src, dst, i):
        def step(d, carry):
            to = (z + d) % NZ

            @pl.when(z >= jnp.minimum(to, NZ - 1 - to))
            def _():
                line_copy(src, dst, i, to, z).wait_send()

            return carry

        lax.fori_loop(1, NZ, step, 0)

    def pair_copy(src, dst, i):
        return send(
            src.at[1 - head], dst.at[head, rows_at(x)], os.at[i], orr.at[i], other * NX + x
        )

    def cross_copies(dst, slot, i):
        return [
            send(dst.at[slot, rows_at(x)], dst.at[slot, rows_at(x)], xs.at[i, d], xr.at[i, d], z * NX + xx)
            for d, xx in enumerate(cross)
        ]

    for read in reads:
        read.wait()
    for part in range(2):
        cols = slice(part * HD, (part + 1) * HD)
        cs[part] = c[:, cols]
        vs[part] = v[:, cols]
    v_pair = pair_copy(vs, vg, 0)
    v_pair.start()
    line_start(cs, cg, 0)
    cg[z] = cs[head]
    vg[head, rows_at(x)] = vs[head]
    v_cross = cross_copies(vg, head, 0)
    for copy in v_cross:
        copy.start()
    loads = [pltpu.make_async_copy(src, w.at[i], ws.at[i]) for i, src in enumerate((wq, wk, wv))]
    for load in loads:
        load.start()

    reflectors(hh, units, updates, products, lowers, inverses)
    for a in range(2):
        px[x, a] = nn3(products[a, 0], products[a, 1])
    p_cross = [
        send(px.at[x], px.at[x], ps.at[d], pr.at[d], z * NX + xx) for d, xx in enumerate(cross)
    ]
    for copy in p_cross:
        copy.start()

    v_pair.wait()
    v_cross2 = cross_copies(vg, 1 - head, 1)
    for copy in v_cross2:
        copy.start()
    row, col = iotas((HD, HD))
    for a in range(2):
        for b in range(2):
            rows = slice(b * HD, (b + 1) * HD)
            for src, dst in ((q, qlocal), (k, klocal)):
                part = src[rows, a * HD : (a + 1) * HD].astype(F32)
                coef = jnp.where(row >= col, nt3(part, units[a, rows]), 0.0)
                dst[a, rows] = part - nn3(coef, updates[a, rows])

    for copy in p_cross:
        copy.wait()
    for a in range(2):
        one = px[0, a]
        two = nn3(one, px[1, a])
        tz[z, a] = nn3(two, nn3(px[2, a], px[3, a])).astype(BF)
        three = nn3(two, px[2, a])
        totals[a] = jnp.where(
            x == 0, identity(), jnp.where(x == 1, one, jnp.where(x == 2, two, three))
        )
    band = pl.ds(pl.multiple_of(x * 32, 32), 32)

    def t_copy(to, source):
        return send(
            tz.at[source, :, band], tz.at[source, :, band], ts.at[to], tr.at[source], to * NX + x
        )

    def t_forward(source):
        return [
            send(
                tz.at[source, :, band],
                tz.at[source, :, band],
                fs.at[source, d],
                fr.at[source, d],
                z * NX + xx,
            )
            for d, xx in enumerate(cross)
        ]

    def t_start(to, carry):
        t_copy(to, z).start()
        return carry

    lax.fori_loop(z + 1, NZ, t_start, 0)

    def t_step(d, carry):
        @pl.when(d <= z)
        def _():
            t_copy(z, z - d).wait_recv()
            for copy in t_forward(z - d):
                copy.start()

        @pl.when(d > 2)
        def _():
            source = z - d + 2
            for copy in t_forward(source):
                copy.wait()
            for a in range(2):
                totals[a] = nn2(tz[source, a], totals[a])

        return carry

    lax.fori_loop(1, jnp.where(z > 0, z + 3, 1), t_step, 0)
    for a in range(2):
        prefixes[a, 0] = totals[a]
        prefixes[a, 1] = nn3(totals[a], products[a, 0])
        for b in range(2):
            rows = slice(b * HD, (b + 1) * HD)
            ks[a, rows] = nt3(klocal[a, rows], prefixes[a, b]).astype(BF)
    k_pair = pair_copy(ks, kg, 1)
    k_pair.start()
    kg[head, rows_at(x)] = ks[head]
    k_cross = cross_copies(kg, head, 2)
    for copy in k_cross:
        copy.start()
    for a in range(2):
        for b in range(2):
            rows = slice(b * HD, (b + 1) * HD)
            qs[a, rows] = nt3(qlocal[a, rows], prefixes[a, b]).astype(BF)
    line_start(qs, qg, 1)
    qg[z] = qs[head]
    for copy in v_cross + v_cross2:
        copy.wait()

    def c_wait(d, carry):
        source = (z + d) % NZ

        @pl.when(source >= low_row)
        def _():
            line_copy(cs, cg, 0, z, source).wait_recv()

        return carry

    lax.fori_loop(1, NZ, c_wait, 0)

    def weigh(t, carry):
        slot = jnp.where(t < NZ - low_row, 0, 1)
        r = jnp.where(slot == 0, t + low_row, t - 1)
        cot = cg[r]
        for j in range(NX):
            rows = slice(j * ROWS, (j + 1) * ROWS)
            gw[t, rows] = nt(vg[slot, rows], cot)
        return carry

    lax.fori_loop(0, 9, weigh, 0)
    k_pair.wait()
    k_cross2 = cross_copies(kg, 1 - head, 3)
    for copy in k_cross2:
        copy.start()

    def t_done(to, carry):
        t_copy(to, z).wait_send()
        return carry

    lax.fori_loop(z + 1, NZ, t_done, 0)
    for copy in k_cross:
        copy.wait()

    top, total, delta = (held.at[z % 4, i] for i in range(3))
    top[...] = jnp.full(top.shape, LOW, F32)
    total[...] = jnp.zeros(total.shape, F32)
    delta[...] = jnp.zeros(delta.shape, F32)
    key_at, query_at = iotas((ROWS, ROWS))

    def join(at, peak, weight, moment):
        old = top[at, :]
        new = jnp.maximum(old, peak)
        keep, take = jnp.exp2(old - new), jnp.exp2(peak - new)
        top[at, :] = new
        total[at, :] = total[at, :] * keep + weight * take
        delta[at, :] = delta[at, :] * keep + moment * take

    def tile_of(r, slot):
        return jnp.where(slot == 0, r - low_row, r + 1)

    def forward_full(r, slot):
        query, t = qg[r], tile_of(r, slot)
        peak = None
        for j in range(NX):
            rows = slice(j * ROWS, (j + 1) * ROWS)
            score = nt(kg[slot, rows], query) * SCALE2
            pt[t, rows] = score
            high = jnp.max(score, axis=0, keepdims=True)
            peak = high if peak is None else jnp.maximum(peak, high)
        weight = moment = jnp.zeros((1, ROWS), F32)
        for j in range(NX):
            rows = slice(j * ROWS, (j + 1) * ROWS)
            p = jnp.exp2(pt[t, rows] - peak)
            pt[t, rows] = p
            weight = weight + jnp.sum(p, axis=0, keepdims=True)
            moment = moment + jnp.sum(p * gw[t, rows], axis=0, keepdims=True)
        peaks[pl.ds(t, 1), :] = peak
        join(pl.ds(r, 1), peak, weight, moment)

    def forward_edge(r, slot):
        t = tile_of(r, slot)

        def scores(j, peak):
            rows = rows_at(j)
            live = key_at + j * ROWS <= query_at + x * ROWS
            score = jnp.where(live, nt(kg[slot, rows], qg[r]) * SCALE2, LOW)
            pt[t, rows] = score
            return jnp.maximum(peak, jnp.max(score, axis=0, keepdims=True))

        peak = lax.fori_loop(0, x + 1, scores, jnp.full((1, ROWS), LOW, F32))

        def sums(j, carry):
            weight, moment = carry
            rows = rows_at(j)
            p = jnp.exp2(pt[t, rows] - peak)
            pt[t, rows] = p
            weight = weight + jnp.sum(p, axis=0, keepdims=True)
            return weight, moment + jnp.sum(p * gw[t, rows], axis=0, keepdims=True)

        nothing = jnp.zeros((1, ROWS), F32)
        weight, moment = lax.fori_loop(0, x + 1, sums, (nothing, nothing))
        peaks[pl.ds(t, 1), :] = peak
        join(pl.ds(r, 1), peak, weight, moment)

    def forward_row(n, carry):
        slot = jnp.where(n < NZ, head, 1 - head)
        key_row = jnp.where(slot == 0, low_row, NZ - 1 - low_row)
        m = n % NZ
        offset = (m + 1) // 2
        r = (z + NZ + jnp.where(m % 2 == 1, offset, -offset)) % NZ

        @pl.when((n < NZ) & (r != z) & (r >= low_row))
        def _():
            line_copy(qs, qg, 1, z, r).wait_recv()

        @pl.when(n == NZ)
        def _():
            for copy in k_cross2:
                copy.wait()

        @pl.when(r > key_row)
        def _():
            forward_full(r, slot)

        @pl.when(r == key_row)
        def _():
            forward_edge(r, slot)

        return carry

    lax.fori_loop(0, 2 * NZ, forward_row, 0)

    half_peers = [(head * 4 + (z + d) % 4) * NX + x for d in range(1, 4)]
    stat_copies = [
        send(held.at[z % 4], held.at[z % 4], ss.at[d], sr.at[d], peer)
        for d, peer in enumerate(half_peers)
    ]
    for copy in stat_copies:
        copy.start()
    line_wait_send(cs, cg, 0)
    line_wait_send(qs, qg, 1)
    dq_acc[...] = jnp.zeros(dq_acc.shape, F32)
    dk_acc[...] = jnp.zeros(dk_acc.shape, F32)
    dv_acc[...] = jnp.zeros(dv_acc.shape, F32)
    for slot in range(2):
        for j in range(NX):
            kt[slot, j] = kg[slot, j * ROWS : (j + 1) * ROWS].T
    for copy in stat_copies:
        copy.wait()
    peak = held[0, 0]
    for i in range(1, 4):
        peak = jnp.maximum(peak, held[i, 0])
    weight = moment = jnp.zeros(peak.shape, F32)
    for i in range(4):
        take = jnp.exp2(held[i, 0] - peak)
        weight = weight + held[i, 1] * take
        moment = moment + held[i, 2] * take
    log_total[...] = peak + jnp.log2(weight)
    delta_row[...] = moment / weight

    def tile(r, slot, j, rows):
        t, at = tile_of(r, slot), pl.ds(r, 1)
        p = pt[t, rows] * jnp.exp2(peaks[pl.ds(t, 1), :] - log_total[at, :])
        grad = (p * (gw[t, rows] - delta_row[at, :])).astype(BF)
        dv_acc[slot, rows] += nn(p.astype(BF), cg[r])
        dk_acc[slot, rows] += nn(grad, qg[r])
        return nn(kt[slot, j], grad)

    def backward_full(r, slot):
        total = None
        for j in range(NX):
            part = tile(r, slot, j, slice(j * ROWS, (j + 1) * ROWS))
            total = part if total is None else total + part
        dq_acc[r] += total

    def backward_edge(r, slot):
        def step(j, carry):
            dq_acc[r] += tile(r, slot, j, rows_at(j))
            return carry

        lax.fori_loop(0, x + 1, step, 0)

    def dq_copy(to, source):
        return send(dqt.at[to], rq.at[source], zs.at[2, to], zr.at[2, source], to * NX + x)

    def backward_row(n, carry):
        slot = jnp.where(n < NZ, 1 - head, head)
        key_row = jnp.where(slot == 0, low_row, NZ - 1 - low_row)
        m = n % NZ
        offset = 4 - (m + 1) // 2
        r = (z + NZ + jnp.where(m % 2 == 1, offset, -offset)) % NZ

        @pl.when(r > key_row)
        def _():
            backward_full(r, slot)

        @pl.when(r == key_row)
        def _():
            backward_edge(r, slot)

        alone = (head == 1) & (r < NZ - 1 - low_row)

        @pl.when((r >= low_row) & ((n >= NZ) != alone))
        def _():
            dqt[r] = (dq_acc[r] * SCALE).astype(BF)

            @pl.when(r != z)
            def _():
                dq_copy(r, z).start()

        @pl.when((n == NZ - 1) | (n == 2 * NZ - 1))
        def _():
            i = n // NZ
            dkv[slot, :, :HD] = (dk_acc[slot] * SCALE).astype(BF)
            dkv[slot, :, HD:] = dv_acc[slot].astype(BF)
            rx[x, i] = dkv[slot, rows_at(x)]
            for copy in kv_copies(i):
                copy.start()

        return carry

    def kv_copies(i):
        slot = jnp.where(i == 0, 1 - head, head)
        return [
            send(dkv.at[slot, rows_at(xx)], rx.at[x, i], xs.at[4 + i, d], xr.at[4 + i, d], z * NX + xx)
            for d, xx in enumerate(cross)
        ]

    lax.fori_loop(0, 2 * NZ, backward_row, 0)

    def summed(i):
        return (rx[0, i].astype(F32) + rx[1, i].astype(F32)) + (
            rx[2, i].astype(F32) + rx[3, i].astype(F32)
        )

    for copy in kv_copies(0):
        copy.wait()
    pair_out[0] = summed(0).astype(BF)
    pair = send(pair_out.at[0], pair_out.at[1], os.at[2], orr.at[2], other * NX + x)
    pair.start()

    rq[z] = dqt[z]

    def dq_wait(d, carry):
        to = (z + d) % NZ

        @pl.when(to >= low_row)
        def _():
            dq_copy(to, z).wait_send()

        @pl.when(z >= jnp.minimum(to, NZ - 1 - to))
        def _():
            dq_copy(z, to).wait_recv()

        @pl.when(z < jnp.minimum(to, NZ - 1 - to))
        def _():
            rq[to] = jnp.zeros(rq.shape[1:], BF)

        return carry

    lax.fori_loop(1, NZ, dq_wait, 0)

    def turn_back(i, a, b, part):
        rows, cols = slice(b * HD, (b + 1) * HD), pl.ds(pl.multiple_of(a * HD, HD), HD)
        back = nn3(part, prefixes[a, b])
        coef = jnp.where(row >= col, nt3(back, updates[a, rows]), 0.0)
        grads[i, rows, cols] = (back - nn3(coef, units[a, rows])).astype(BF)

    for a in range(2):
        total = rq[4 * a].astype(F32)
        for i in range(1, 4):
            total = total + rq[4 * a + i].astype(F32)
        total = total.T
        for b in range(2):
            turn_back(0, a, b, total[b * HD : (b + 1) * HD])
    for copy in kv_copies(1):
        copy.wait()

    def finish(a):
        grads[2, :, pl.ds(pl.multiple_of(a * HD, HD), HD)] = kv[a, :, HD:].astype(BF)
        for b in range(2):
            turn_back(1, a, b, kv[a, b * HD : (b + 1) * HD, :HD])

    kv[head] = summed(1)
    finish(head)
    pair.wait()
    kv[1 - head] = pair_out[1].astype(F32)
    finish(1 - head)
    for load in loads:
        load.wait()

    def columns(block):
        at = pl.ds(pl.multiple_of(block * 512, 512), 512)
        return (
            nt(grads[0], w[0, at, :]) + nt(grads[1], w[1, at, :]) + nt(grads[2], w[2, at, :])
        )

    half = ROWS // 2
    blocks = [(y + 2) % 4, above, below, y]
    swaps = []

    def give(i):
        mine[i] = columns(blocks[i] * 2 + 1 - core).astype(BF)
        swap = send(mine.at[i], theirs.at[i], ms.at[i], mr.at[i], mate, "head")
        swap.start()
        swaps.append(swap)

    def take(i):
        part = columns(blocks[i] * 2 + core)
        swaps[i].wait()
        return part + theirs[i].astype(F32)

    def hop(i, src, dst, to):
        copy = send(src, dst, ys.at[i], yr.at[i], to * 2 + core, "head")
        copy.start()
        return copy

    give(0)
    give(1)
    relay[0] = take(0).astype(BF)
    up = hop(0, relay.at[0, :half], landed.at[0, :half], above)
    down = hop(1, relay.at[0, half:], landed.at[0, half:], below)
    give(2)
    part = take(1)
    joined[0] = part[:half]
    relay[1, half:] = part[half:].astype(BF)
    hops = [hop(2, relay.at[1, half:], landed.at[1, half:], above)]
    give(3)
    part = take(2)
    joined[1] = part[half:]
    relay[2, :half] = part[:half].astype(BF)
    hops.append(hop(3, relay.at[2, :half], landed.at[2, :half], below))
    up.wait()
    relay[1, :half] = (joined[0] + landed[0, :half].astype(F32)).astype(BF)
    hops.append(hop(4, relay.at[1, :half], landed.at[1, :half], above))
    down.wait()
    relay[2, half:] = (joined[1] + landed[0, half:].astype(F32)).astype(BF)
    hops.append(hop(5, relay.at[2, half:], landed.at[2, half:], below))
    out[...] = take(3)
    for copy in hops:
        copy.wait()
    out[...] = out[...] + (landed[1].astype(F32) + landed[2].astype(F32))


def on_device(query, key, value, householder, cotangent, w_query, w_key, w_value):
    dma = pltpu.SemaphoreType.DMA
    own, own32 = ((2, ROWS, HD), BF), ((2, ROWS, HD), F32)
    lines, keys = ((NZ, ROWS, HD), BF), ((2, NX * ROWS, HD), BF)
    square = (HD, HD)
    stat = ((NZ, ROWS), F32)
    acc = ((2, NX * ROWS, HD), F32)
    block = (ROWS, 2 * HD)
    wide = (ROWS, 512)
    scratch = [(block, BF)] * 5 + [
        lines, lines, keys, keys, own32, own32, ((2, 2) + square, F32),
        own, own, own, own, ((NX, 2) + square, F32), ((NZ, 2) + square, BF), own32, own32,
        ((2, 2) + square, F32), ((4,) + square, F32), ((4,) + square, F32), ((2,) + square, F32),
        ((9, NX * ROWS, ROWS), F32), ((9, NX * ROWS, ROWS), F32), ((16, ROWS), F32), ((4, 3, NZ, ROWS), F32), stat, stat,
        ((2, NX, HD, ROWS), BF), ((NZ, HD, ROWS), F32), acc, acc,
        ((NZ, HD, ROWS), BF), ((2, NX * ROWS, 2 * HD), BF), ((NZ, HD, ROWS), BF),
        ((NX, 2) + block, BF), ((2,) + block, BF), ((2,) + block, F32),
        ((3, 4096, ROWS), BF), ((3,) + block, BF),
        ((4,) + wide, BF), ((4,) + wide, BF), ((3,) + wide, BF), ((3,) + wide, BF),
        ((2, ROWS // 2, 512), F32),
    ]
    sems = [
        (3, 8), (3, 8), (6, 3), (6, 3), (3,), (3,), (8,), (8,), (8, 3), (8, 3), (3,), (3,),
        (3,), (3,), (3,), (5,), (4,), (4,), (6,), (6,),
    ]
    vmem = pl.BlockSpec(memory_space=pltpu.VMEM)
    return pl.pallas_call(
        whole_kernel,
        out_shape=jax.ShapeDtypeStruct(wide, F32),
        in_specs=[pl.BlockSpec(memory_space=pl.ANY)] * 8,
        out_specs=vmem,
        scratch_shapes=[pltpu.VMEM(*s) for s in scratch] + [dma(s) for s in sems],
        compiler_params=pltpu.CompilerParams(
            vmem_limit_bytes=VMEM_BYTES, collective_id=0, has_side_effects=True
        ),
    )(householder, query, key, value, cotangent, w_query, w_key, w_value)


def solution(mesh):
    return jax.shard_map(
        on_device,
        mesh=mesh,
        in_specs=(P("ctx", "head"),) * 5 + (P(None, "head"),) * 3,
        out_specs=P("ctx", "head"),
        check_vma=False,
    )
```

```python
import math

import jax
import jax.numpy as jnp
from jax import lax
from jax.experimental import pallas as pl
from jax.experimental.pallas import tpu as pltpu
from jax.sharding import PartitionSpec as P

MESH = pl.DeviceIdType.MESH
BF = jnp.bfloat16
F32 = jnp.float32
ROWS = 256
HD = 128
NZ, NX = 8, 4
SCALE = HD**-0.5
SCALE2 = SCALE * math.log2(math.e)
VMEM_BYTES = 56 * 1024 * 1024
LOW = -1e30


def nn(a, b):
    return lax.dot_general(a, b, (((1,), (0,)), ((), ())), preferred_element_type=F32)


def nt(a, b):
    return lax.dot_general(a, b, (((1,), (1,)), ((), ())), preferred_element_type=F32)


def split(a):
    high = a.astype(BF)
    return high, (a - high.astype(F32)).astype(BF)


def nn3(a, b):
    ah, al = split(a)
    bh, bl = split(b)
    return nn(ah, bh) + (nn(al, bh) + nn(ah, bl))


def nt3(a, b):
    ah, al = split(a)
    bh, bl = split(b)
    return nt(ah, bh) + (nt(al, bh) + nt(ah, bl))


def nn2(a, b):
    bh, bl = split(b)
    return nn(a, bh) + nn(a, bl)


def iotas(shape):
    return lax.broadcasted_iota(jnp.int32, shape, 0), lax.broadcasted_iota(jnp.int32, shape, 1)


def identity():
    row, col = iotas((HD, HD))
    return jnp.where(row == col, 1.0, 0.0).astype(F32)


def place():
    me = lax.axis_index("ctx")
    return me // NX, me % NX


def send(src, dst, send_sem, recv_sem, peer, axis="ctx"):
    return pltpu.make_async_remote_copy(
        src_ref=src,
        dst_ref=dst,
        send_sem=send_sem,
        recv_sem=recv_sem,
        device_id={axis: peer},
        device_id_type=MESH,
    )


def reflectors(hh, units, updates, products, lowers, inverses):
    row, col = iotas((HD, HD))
    chunks = [(a, b, slice(b * HD, (b + 1) * HD)) for a in range(2) for b in range(2)]
    for i, (a, b, rows) in enumerate(chunks):
        vec = hh[rows, a * HD : (a + 1) * HD].astype(F32)
        unit = vec * lax.rsqrt(jnp.sum(vec * vec, axis=1, keepdims=True) + 1e-6)
        lower = 2.0 * jnp.where(row > col, nt3(unit, unit), 0.0)
        units[a, rows] = unit
        lowers[i] = lower
        inverses[i] = identity() - jnp.where(row // 2 == col // 2, lower, 0.0)

    def join(level, carry):
        row_part, col_part = lax.shift_right_logical(row, level), lax.shift_right_logical(col, level)
        pick = (row_part == col_part + 1) & ((col_part & 1) == 0)
        for i in range(4):
            inverse = inverses[i]
            inner = nn3(jnp.where(pick, lowers[i], 0.0), inverse)
            inverses[i] = inverse - nn3(inverse, inner)
        return carry

    lax.fori_loop(1, 7, join, 0)
    for i, (a, b, rows) in enumerate(chunks):
        unit, inverse = units[a, rows], inverses[i]
        updates[a, rows] = 2.0 * nn3(inverse, unit)
        turned = 2.0 * nt3(unit.T, inverse)
        products[a, b] = identity() - nn3(turned, unit)


def rows_at(block):
    return pl.ds(pl.multiple_of(block * ROWS, ROWS), ROWS)


def whole_kernel(
    hh_in, q_in, k_in, v_in, c_in, wq, wk, wv,
    out,
    hh, q, k, v, c, qg, cg, kg, vg, units, updates, prefixes,
    qs, ks, cs, vs, px, tz, qlocal, klocal, products, lowers, inverses, totals,
    gw, pt, peaks, held, log_total, delta_row,
    kt, dq_acc, dk_acc, dv_acc, dqt, dkv, rq, rx, pair_out, kv,
    w, grads, mine, theirs, relay, landed, joined,
    zs, zr, xs, xr, ps, pr, ts, tr, fs, fr, os, orr, ss, sr, ws, ins, ms, mr, ys, yr,
):
    z, x = place()
    me = lax.axis_index("head")
    y, core = me // 2, me % 2
    mate = y * 2 + 1 - core
    head = z // 4
    low_row = jnp.minimum(z, NZ - 1 - z)
    other = NZ - 1 - z
    line = [(z + d) % NZ for d in range(1, NZ)]
    cross = [(x + d) % NX for d in range(1, NX)]
    above, below = (y + 1) % 4, (y + 3) % 4
    pairs = ((c_in, c), (v_in, v), (hh_in, hh), (q_in, q), (k_in, k))
    reads = [pltpu.make_async_copy(src, dst, ins.at[i]) for i, (src, dst) in enumerate(pairs)]
    for read in reads:
        read.start()
    barrier = pltpu.get_barrier_semaphore()
    peers = [{"ctx": zz * NX + x} for zz in line] + [{"ctx": z * NX + xx} for xx in cross]
    peers = peers + [{"head": mate}] + [{"head": yy * 2 + core} for yy in (above, below)]
    for peer in peers:
        pl.semaphore_signal(barrier, inc=1, device_id=peer, device_id_type=MESH)
    pl.semaphore_wait(barrier, len(peers))

    def line_copy(src, dst, i, to, source):
        return send(src.at[to // 4], dst.at[source], zs.at[i, to], zr.at[i, source], to * NX + x)

    def line_start(src, dst, i):
        def step(d, carry):
            to = (z + d) % NZ

            @pl.when(z >= jnp.minimum(to, NZ - 1 - to))
            def _():
                line_copy(src, dst, i, to, z).start()

            return carry

        lax.fori_loop(1, NZ, step, 0)

    def line_wait_send(src, dst, i):
        def step(d, carry):
            to = (z + d) % NZ

            @pl.when(z >= jnp.minimum(to, NZ - 1 - to))
            def _():
                line_copy(src, dst, i, to, z).wait_send()

            return carry

        lax.fori_loop(1, NZ, step, 0)

    def pair_copy(src, dst, i):
        return send(
            src.at[1 - head], dst.at[head, rows_at(x)], os.at[i], orr.at[i], other * NX + x
        )

    def cross_copies(dst, slot, i):
        return [
            send(dst.at[slot, rows_at(x)], dst.at[slot, rows_at(x)], xs.at[i, d], xr.at[i, d], z * NX + xx)
            for d, xx in enumerate(cross)
        ]

    for read in reads:
        read.wait()
    for part in range(2):
        cols = slice(part * HD, (part + 1) * HD)
        cs[part] = c[:, cols]
        vs[part] = v[:, cols]
    v_pair = pair_copy(vs, vg, 0)
    v_pair.start()
    line_start(cs, cg, 0)
    cg[z] = cs[head]
    vg[head, rows_at(x)] = vs[head]
    v_cross = cross_copies(vg, head, 0)
    for copy in v_cross:
        copy.start()
    loads = [pltpu.make_async_copy(src, w.at[i], ws.at[i]) for i, src in enumerate((wq, wk, wv))]
    for load in loads:
        load.start()

    reflectors(hh, units, updates, products, lowers, inverses)
    for a in range(2):
        px[x, a] = nn3(products[a, 0], products[a, 1])
    p_cross = [
        send(px.at[x], px.at[x], ps.at[d], pr.at[d], z * NX + xx) for d, xx in enumerate(cross)
    ]
    for copy in p_cross:
        copy.start()

    v_pair.wait()
    v_cross2 = cross_copies(vg, 1 - head, 1)
    for copy in v_cross2:
        copy.start()
    row, col = iotas((HD, HD))
    for a in range(2):
        for b in range(2):
            rows = slice(b * HD, (b + 1) * HD)
            for src, dst in ((q, qlocal), (k, klocal)):
                part = src[rows, a * HD : (a + 1) * HD].astype(F32)
                coef = jnp.where(row >= col, nt3(part, units[a, rows]), 0.0)
                dst[a, rows] = part - nn3(coef, updates[a, rows])

    for copy in p_cross:
        copy.wait()
    for a in range(2):
        one = px[0, a]
        two = nn3(one, px[1, a])
        tz[z, a] = nn3(two, nn3(px[2, a], px[3, a])).astype(BF)
        three = nn3(two, px[2, a])
        totals[a] = jnp.where(
            x == 0, identity(), jnp.where(x == 1, one, jnp.where(x == 2, two, three))
        )
    band = pl.ds(pl.multiple_of(x * 32, 32), 32)

    def t_copy(to, source):
        return send(
            tz.at[source, :, band], tz.at[source, :, band], ts.at[to], tr.at[source], to * NX + x
        )

    def t_forward(source):
        return [
            send(
                tz.at[source, :, band],
                tz.at[source, :, band],
                fs.at[source, d],
                fr.at[source, d],
                z * NX + xx,
            )
            for d, xx in enumerate(cross)
        ]

    def t_start(to, carry):
        t_copy(to, z).start()
        return carry

    lax.fori_loop(z + 1, NZ, t_start, 0)

    def t_step(d, carry):
        @pl.when(d <= z)
        def _():
            t_copy(z, z - d).wait_recv()
            for copy in t_forward(z - d):
                copy.start()

        @pl.when(d > 4)
        def _():
            source = z - d + 4
            for copy in t_forward(source):
                copy.wait()
            for a in range(2):
                totals[a] = nn2(tz[source, a], totals[a])

        return carry

    lax.fori_loop(1, jnp.where(z > 0, z + 5, 1), t_step, 0)
    for a in range(2):
        prefixes[a, 0] = totals[a]
        prefixes[a, 1] = nn3(totals[a], products[a, 0])
        for b in range(2):
            rows = slice(b * HD, (b + 1) * HD)
            ks[a, rows] = nt3(klocal[a, rows], prefixes[a, b]).astype(BF)
    k_pair = pair_copy(ks, kg, 1)
    k_pair.start()
    kg[head, rows_at(x)] = ks[head]
    k_cross = cross_copies(kg, head, 2)
    for copy in k_cross:
        copy.start()
    for a in range(2):
        for b in range(2):
            rows = slice(b * HD, (b + 1) * HD)
            qs[a, rows] = nt3(qlocal[a, rows], prefixes[a, b]).astype(BF)
    line_start(qs, qg, 1)
    qg[z] = qs[head]
    for copy in v_cross + v_cross2:
        copy.wait()

    def c_wait(d, carry):
        source = (z + d) % NZ

        @pl.when(source >= low_row)
        def _():
            line_copy(cs, cg, 0, z, source).wait_recv()

        return carry

    lax.fori_loop(1, NZ, c_wait, 0)

    def weigh(t, carry):
        slot = jnp.where(t < NZ - low_row, 0, 1)
        r = jnp.where(slot == 0, t + low_row, t - 1)
        cot = cg[r]
        for j in range(NX):
            rows = slice(j * ROWS, (j + 1) * ROWS)
            gw[t, rows] = nt(vg[slot, rows], cot)
        return carry

    lax.fori_loop(0, 9, weigh, 0)
    k_pair.wait()
    k_cross2 = cross_copies(kg, 1 - head, 3)
    for copy in k_cross2:
        copy.start()

    def t_done(to, carry):
        t_copy(to, z).wait_send()
        return carry

    lax.fori_loop(z + 1, NZ, t_done, 0)
    for copy in k_cross:
        copy.wait()

    top, total, delta = (held.at[z % 4, i] for i in range(3))
    top[...] = jnp.full(top.shape, LOW, F32)
    total[...] = jnp.zeros(total.shape, F32)
    delta[...] = jnp.zeros(delta.shape, F32)
    key_at, query_at = iotas((ROWS, ROWS))

    def join(at, peak, weight, moment):
        old = top[at, :]
        new = jnp.maximum(old, peak)
        keep, take = jnp.exp2(old - new), jnp.exp2(peak - new)
        top[at, :] = new
        total[at, :] = total[at, :] * keep + weight * take
        delta[at, :] = delta[at, :] * keep + moment * take

    def tile_of(r, slot):
        return jnp.where(slot == 0, r - low_row, r + 1)

    def forward_full(r, slot):
        query, t = qg[r], tile_of(r, slot)
        peak = None
        for j in range(NX):
            rows = slice(j * ROWS, (j + 1) * ROWS)
            score = nt(kg[slot, rows], query) * SCALE2
            pt[t, rows] = score
            high = jnp.max(score, axis=0, keepdims=True)
            peak = high if peak is None else jnp.maximum(peak, high)
        weight = moment = jnp.zeros((1, ROWS), F32)
        for j in range(NX):
            rows = slice(j * ROWS, (j + 1) * ROWS)
            p = jnp.exp2(pt[t, rows] - peak)
            pt[t, rows] = p
            weight = weight + jnp.sum(p, axis=0, keepdims=True)
            moment = moment + jnp.sum(p * gw[t, rows], axis=0, keepdims=True)
        peaks[pl.ds(t, 1), :] = peak
        join(pl.ds(r, 1), peak, weight, moment)

    def forward_edge(r, slot):
        t = tile_of(r, slot)

        def scores(j, peak):
            rows = rows_at(j)
            live = key_at + j * ROWS <= query_at + x * ROWS
            score = jnp.where(live, nt(kg[slot, rows], qg[r]) * SCALE2, LOW)
            pt[t, rows] = score
            return jnp.maximum(peak, jnp.max(score, axis=0, keepdims=True))

        peak = lax.fori_loop(0, x + 1, scores, jnp.full((1, ROWS), LOW, F32))

        def sums(j, carry):
            weight, moment = carry
            rows = rows_at(j)
            p = jnp.exp2(pt[t, rows] - peak)
            pt[t, rows] = p
            weight = weight + jnp.sum(p, axis=0, keepdims=True)
            return weight, moment + jnp.sum(p * gw[t, rows], axis=0, keepdims=True)

        nothing = jnp.zeros((1, ROWS), F32)
        weight, moment = lax.fori_loop(0, x + 1, sums, (nothing, nothing))
        peaks[pl.ds(t, 1), :] = peak
        join(pl.ds(r, 1), peak, weight, moment)

    def forward_row(n, carry):
        slot = jnp.where(n < NZ, head, 1 - head)
        key_row = jnp.where(slot == 0, low_row, NZ - 1 - low_row)
        m = n % NZ
        offset = (m + 1) // 2
        r = (z + NZ + jnp.where(m % 2 == 1, offset, -offset)) % NZ

        @pl.when((n < NZ) & (r != z) & (r >= low_row))
        def _():
            line_copy(qs, qg, 1, z, r).wait_recv()

        @pl.when(n == NZ)
        def _():
            for copy in k_cross2:
                copy.wait()

        @pl.when(r > key_row)
        def _():
            forward_full(r, slot)

        @pl.when(r == key_row)
        def _():
            forward_edge(r, slot)

        return carry

    lax.fori_loop(0, 2 * NZ, forward_row, 0)

    half_peers = [(head * 4 + (z + d) % 4) * NX + x for d in range(1, 4)]
    stat_copies = [
        send(held.at[z % 4], held.at[z % 4], ss.at[d], sr.at[d], peer)
        for d, peer in enumerate(half_peers)
    ]
    for copy in stat_copies:
        copy.start()
    line_wait_send(cs, cg, 0)
    line_wait_send(qs, qg, 1)
    dq_acc[...] = jnp.zeros(dq_acc.shape, F32)
    dk_acc[...] = jnp.zeros(dk_acc.shape, F32)
    dv_acc[...] = jnp.zeros(dv_acc.shape, F32)
    for slot in range(2):
        for j in range(NX):
            kt[slot, j] = kg[slot, j * ROWS : (j + 1) * ROWS].T
    for copy in stat_copies:
        copy.wait()
    peak = held[0, 0]
    for i in range(1, 4):
        peak = jnp.maximum(peak, held[i, 0])
    weight = moment = jnp.zeros(peak.shape, F32)
    for i in range(4):
        take = jnp.exp2(held[i, 0] - peak)
        weight = weight + held[i, 1] * take
        moment = moment + held[i, 2] * take
    log_total[...] = peak + jnp.log2(weight)
    delta_row[...] = moment / weight

    def tile(r, slot, j, rows):
        t, at = tile_of(r, slot), pl.ds(r, 1)
        p = pt[t, rows] * jnp.exp2(peaks[pl.ds(t, 1), :] - log_total[at, :])
        grad = (p * (gw[t, rows] - delta_row[at, :])).astype(BF)
        dv_acc[slot, rows] += nn(p.astype(BF), cg[r])
        dk_acc[slot, rows] += nn(grad, qg[r])
        return nn(kt[slot, j], grad)

    def backward_full(r, slot):
        total = None
        for j in range(NX):
            part = tile(r, slot, j, slice(j * ROWS, (j + 1) * ROWS))
            total = part if total is None else total + part
        dq_acc[r] += total

    def backward_edge(r, slot):
        def step(j, carry):
            dq_acc[r] += tile(r, slot, j, rows_at(j))
            return carry

        lax.fori_loop(0, x + 1, step, 0)

    def dq_copy(to, source):
        return send(dqt.at[to], rq.at[source], zs.at[2, to], zr.at[2, source], to * NX + x)

    def backward_row(n, carry):
        slot = jnp.where(n < NZ, 1 - head, head)
        key_row = jnp.where(slot == 0, low_row, NZ - 1 - low_row)
        m = n % NZ
        offset = 4 - (m + 1) // 2
        r = (z + NZ + jnp.where(m % 2 == 1, offset, -offset)) % NZ

        @pl.when(r > key_row)
        def _():
            backward_full(r, slot)

        @pl.when(r == key_row)
        def _():
            backward_edge(r, slot)

        alone = (head == 1) & (r < NZ - 1 - low_row)

        @pl.when((r >= low_row) & ((n >= NZ) != alone))
        def _():
            dqt[r] = (dq_acc[r] * SCALE).astype(BF)

            @pl.when(r != z)
            def _():
                dq_copy(r, z).start()

        @pl.when((n == NZ - 1) | (n == 2 * NZ - 1))
        def _():
            i = n // NZ
            dkv[slot, :, :HD] = (dk_acc[slot] * SCALE).astype(BF)
            dkv[slot, :, HD:] = dv_acc[slot].astype(BF)
            rx[x, i] = dkv[slot, rows_at(x)]
            for copy in kv_copies(i):
                copy.start()

        return carry

    def kv_copies(i):
        slot = jnp.where(i == 0, 1 - head, head)
        return [
            send(dkv.at[slot, rows_at(xx)], rx.at[x, i], xs.at[4 + i, d], xr.at[4 + i, d], z * NX + xx)
            for d, xx in enumerate(cross)
        ]

    lax.fori_loop(0, 2 * NZ, backward_row, 0)

    def summed(i):
        return (rx[0, i].astype(F32) + rx[1, i].astype(F32)) + (
            rx[2, i].astype(F32) + rx[3, i].astype(F32)
        )

    for copy in kv_copies(0):
        copy.wait()
    pair_out[0] = summed(0).astype(BF)
    pair = send(pair_out.at[0], pair_out.at[1], os.at[2], orr.at[2], other * NX + x)
    pair.start()

    rq[z] = dqt[z]

    def dq_wait(d, carry):
        to = (z + d) % NZ

        @pl.when(to >= low_row)
        def _():
            dq_copy(to, z).wait_send()

        @pl.when(z >= jnp.minimum(to, NZ - 1 - to))
        def _():
            dq_copy(z, to).wait_recv()

        @pl.when(z < jnp.minimum(to, NZ - 1 - to))
        def _():
            rq[to] = jnp.zeros(rq.shape[1:], BF)

        return carry

    lax.fori_loop(1, NZ, dq_wait, 0)

    def turn_back(i, a, b, part):
        rows, cols = slice(b * HD, (b + 1) * HD), pl.ds(pl.multiple_of(a * HD, HD), HD)
        back = nn3(part, prefixes[a, b])
        coef = jnp.where(row >= col, nt3(back, updates[a, rows]), 0.0)
        grads[i, rows, cols] = (back - nn3(coef, units[a, rows])).astype(BF)

    for a in range(2):
        total = rq[4 * a].astype(F32)
        for i in range(1, 4):
            total = total + rq[4 * a + i].astype(F32)
        total = total.T
        for b in range(2):
            turn_back(0, a, b, total[b * HD : (b + 1) * HD])
    for copy in kv_copies(1):
        copy.wait()

    def finish(a):
        grads[2, :, pl.ds(pl.multiple_of(a * HD, HD), HD)] = kv[a, :, HD:].astype(BF)
        for b in range(2):
            turn_back(1, a, b, kv[a, b * HD : (b + 1) * HD, :HD])

    kv[head] = summed(1)
    finish(head)
    pair.wait()
    kv[1 - head] = pair_out[1].astype(F32)
    finish(1 - head)
    for load in loads:
        load.wait()

    def columns(block):
        at = pl.ds(pl.multiple_of(block * 512, 512), 512)
        return (
            nt(grads[0], w[0, at, :]) + nt(grads[1], w[1, at, :]) + nt(grads[2], w[2, at, :])
        )

    half = ROWS // 2
    blocks = [(y + 2) % 4, above, below, y]
    swaps = []

    def give(i):
        mine[i] = columns(blocks[i] * 2 + 1 - core).astype(BF)
        swap = send(mine.at[i], theirs.at[i], ms.at[i], mr.at[i], mate, "head")
        swap.start()
        swaps.append(swap)

    def take(i):
        part = columns(blocks[i] * 2 + core)
        swaps[i].wait()
        return part + theirs[i].astype(F32)

    def hop(i, src, dst, to):
        copy = send(src, dst, ys.at[i], yr.at[i], to * 2 + core, "head")
        copy.start()
        return copy

    give(0)
    give(1)
    relay[0] = take(0).astype(BF)
    up = hop(0, relay.at[0, :half], landed.at[0, :half], above)
    down = hop(1, relay.at[0, half:], landed.at[0, half:], below)
    give(2)
    part = take(1)
    joined[0] = part[:half]
    relay[1, half:] = part[half:].astype(BF)
    hops = [hop(2, relay.at[1, half:], landed.at[1, half:], above)]
    give(3)
    part = take(2)
    joined[1] = part[half:]
    relay[2, :half] = part[:half].astype(BF)
    hops.append(hop(3, relay.at[2, :half], landed.at[2, :half], below))
    up.wait()
    relay[1, :half] = (joined[0] + landed[0, :half].astype(F32)).astype(BF)
    hops.append(hop(4, relay.at[1, :half], landed.at[1, :half], above))
    down.wait()
    relay[2, half:] = (joined[1] + landed[0, half:].astype(F32)).astype(BF)
    hops.append(hop(5, relay.at[2, half:], landed.at[2, half:], below))
    out[...] = take(3)
    for copy in hops:
        copy.wait()
    out[...] = out[...] + (landed[1].astype(F32) + landed[2].astype(F32))


def on_device(query, key, value, householder, cotangent, w_query, w_key, w_value):
    dma = pltpu.SemaphoreType.DMA
    own, own32 = ((2, ROWS, HD), BF), ((2, ROWS, HD), F32)
    lines, keys = ((NZ, ROWS, HD), BF), ((2, NX * ROWS, HD), BF)
    square = (HD, HD)
    stat = ((NZ, ROWS), F32)
    acc = ((2, NX * ROWS, HD), F32)
    block = (ROWS, 2 * HD)
    wide = (ROWS, 512)
    scratch = [(block, BF)] * 5 + [
        lines, lines, keys, keys, own32, own32, ((2, 2) + square, F32),
        own, own, own, own, ((NX, 2) + square, F32), ((NZ, 2) + square, BF), own32, own32,
        ((2, 2) + square, F32), ((4,) + square, F32), ((4,) + square, F32), ((2,) + square, F32),
        ((9, NX * ROWS, ROWS), F32), ((9, NX * ROWS, ROWS), F32), ((16, ROWS), F32), ((4, 3, NZ, ROWS), F32), stat, stat,
        ((2, NX, HD, ROWS), BF), ((NZ, HD, ROWS), F32), acc, acc,
        ((NZ, HD, ROWS), BF), ((2, NX * ROWS, 2 * HD), BF), ((NZ, HD, ROWS), BF),
        ((NX, 2) + block, BF), ((2,) + block, BF), ((2,) + block, F32),
        ((3, 4096, ROWS), BF), ((3,) + block, BF),
        ((4,) + wide, BF), ((4,) + wide, BF), ((3,) + wide, BF), ((3,) + wide, BF),
        ((2, ROWS // 2, 512), F32),
    ]
    sems = [
        (3, 8), (3, 8), (6, 3), (6, 3), (3,), (3,), (8,), (8,), (8, 3), (8, 3), (3,), (3,),
        (3,), (3,), (3,), (5,), (4,), (4,), (6,), (6,),
    ]
    vmem = pl.BlockSpec(memory_space=pltpu.VMEM)
    return pl.pallas_call(
        whole_kernel,
        out_shape=jax.ShapeDtypeStruct(wide, F32),
        in_specs=[pl.BlockSpec(memory_space=pl.ANY)] * 8,
        out_specs=vmem,
        scratch_shapes=[pltpu.VMEM(*s) for s in scratch] + [dma(s) for s in sems],
        compiler_params=pltpu.CompilerParams(
            vmem_limit_bytes=VMEM_BYTES, collective_id=0, has_side_effects=True
        ),
    )(householder, query, key, value, cotangent, w_query, w_key, w_value)


def solution(mesh):
    return jax.shard_map(
        on_device,
        mesh=mesh,
        in_specs=(P("ctx", "head"),) * 5 + (P(None, "head"),) * 3,
        out_specs=P("ctx", "head"),
        check_vma=False,
    )
```
